256 devices in a mesh: leaf: 32 (over y, x, core), lobe: 8 (over z).
Axes of the slice: x: 4, y: 4, z: 8, core: 2. Of those that a mesh axis runs over, the one named last changes fastest.
Arguments:
- base_velocity: float32 [3, 512, 65536], P(None, None, ('leaf', 'lobe')), may hold values from -6 to 6
- adjoint_velocity: float32 [3, 512, 65536], P(None, None, ('leaf', 'lobe')), may hold values from -6 to 6
- element_size: float32 [65536], P(('leaf', 'lobe')), may hold values from 0.5 to 2
- link_slot: int32 [32768], P(('leaf', 'lobe')), may hold values from -1 to 511, as said below
Outputs:
- adjoint_out: float32 [3, 512, 65536], P(None, None, ('leaf', 'lobe'))
- pressure: float32 [512, 65536], P(None, ('leaf', 'lobe'))
The draws below stay inside these ranges and needn't reach their ends.
Inputs may be any that keep to these rules, and one draw needn't show every extreme that they name: `link_slot`: within one lobe index, row b * 4 + c of leaf index a is >= 0 exactly when row a * 4 + c of leaf index b is; rows naming the device's own leaf index are -1; every row naming leaf index a XOR 1 is >= 0. The values >= 0 of one device are distinct; each names element s % 256 and face 2 + s // 256.
All inputs are finite; a program needn't handle non-finite values.
Results may differ from the reference program's by a relative error of at most 0.0001.
Values sent between devices are 32-bit elements; how exact they have to be, the bound alone decides.
A program may use at most 128 MiB of HBM per device.

```python
import math
import jax
import jax.numpy as jnp
import numpy as np
from jax import lax

NP = 8
E_DEV = 256
CAP = 4
STEPS = 2
ELEMS = 65536
N_LEAF = 32
N_LOBE = 8


def draw_link_slot(key, part):
    key = jax.random.fold_in(key, 7)
    pair_key, slot_key = jax.random.split(key)
    coin_flip = jax.random.randint(pair_key, (N_LOBE, N_LEAF, N_LEAF, CAP), 0, 2).astype(jnp.int32)
    leaf_rows = jnp.arange(N_LEAF, dtype=jnp.int32)[:, None]
    leaf_cols = jnp.arange(N_LEAF, dtype=jnp.int32)[None, :]
    upper_mask = (leaf_rows < leaf_cols)[None, :, :, None]
    linked = jnp.where(upper_mask, coin_flip, jnp.transpose(coin_flip, (0, 2, 1, 3)))
    buddy_mask = (leaf_cols == jnp.bitwise_xor(leaf_rows, 1))[None, :, :, None]
    linked = jnp.where(buddy_mask, 1, linked)
    linked = jnp.where((leaf_rows == leaf_cols)[None, :, :, None], 0, linked)
    linked = jnp.transpose(linked, (1, 0, 2, 3)).reshape(N_LEAF * N_LOBE, N_LEAF * CAP)
    slot_total = 2 * E_DEV
    device_count = N_LEAF * N_LOBE
    device_keys = jax.random.split(slot_key, device_count)
    orders = jax.vmap(lambda one_key: jax.random.permutation(one_key, slot_total))(device_keys).astype(jnp.int32)
    device_rows = jnp.arange(device_count, dtype=jnp.int32)
    forced_place = jnp.bitwise_xor(device_rows // N_LOBE, 1) * CAP
    top_place = jnp.argmax((orders == slot_total - 1).astype(jnp.int32), axis=1).astype(jnp.int32)
    at_forced = orders[device_rows, forced_place]
    orders = orders.at[device_rows, top_place].set(at_forced)
    orders = orders.at[device_rows, forced_place].set(slot_total - 1)
    chosen = orders[:, :N_LEAF * CAP]
    return jnp.where(linked == 1, chosen, -1).reshape(-1).astype(jnp.int32)


def level_of(own_key, shape, cuts, smallest, high):
    factor_of, own = 1.0, jax.random.fold_in(own_key, 6)
    for axis_at, blocks in cuts:
        heights = jnp.exp(jax.random.uniform(jax.random.fold_in(own, axis_at), (blocks,), jnp.float32, smallest / len(cuts), high / len(cuts)))
        factor_of = factor_of * jnp.repeat(heights, shape[axis_at] // blocks).reshape([-1 if axis == axis_at else 1 for axis in range(len(shape))])
    return factor_of


def scatter_about(key, shape, width, limit, pieces=(), held_as=jnp.bfloat16):
    values = jax.random.normal(key, shape, jnp.float32) * width
    if len(pieces) > 0:
        values = level_of(key, shape, pieces, -0.22, 0.18) * values
    return jnp.clip(values, min=-limit, max=limit).astype(held_as)


def setup_inputs(seed: int = 0) -> dict:
    key_of = jax.random.split(jax.random.key(seed), 5)
    return {
        "base_velocity": scatter_about(key_of[0], (3, NP * NP * NP, ELEMS), 1.0, 6.0, ((2, 256),), jnp.float32),
        "adjoint_velocity": scatter_about(key_of[1], (3, NP * NP * NP, ELEMS), 1.0, 6.0, ((2, 256),), jnp.float32),
        "element_size": jnp.clip(jnp.exp(math.log(2.0) - 1.3862944 * jax.random.uniform(key_of[2], (ELEMS,), jnp.float32) ** level_of(key_of[2], (ELEMS,), ((0, 256),), -0.2, 0.2)), 0.5, 2.0),
        "link_slot": draw_link_slot(jax.random.fold_in(key_of[4], 71), 0),
    }


time_step = 0.01
viscosity = 0.002
penalty = 0.5
shift_term = 1.0

def legendre_columns(points, degree):
    table = np.zeros((points.shape[0], degree + 1))
    table[:, 0] = 1.0
    table[:, 1] = points
    for order in range(2, degree + 1):
        table[:, order] = ((2 * order - 1) * points * table[:, order - 1] - (order - 1) * table[:, order - 2]) / order
    return table

def node_tables():
    degree = NP - 1
    node_points = np.cos(np.pi * np.arange(degree + 1) / degree)
    for sweep in range(100):
        table = legendre_columns(node_points, degree)
        node_points = node_points - (node_points * table[:, degree] - table[:, degree - 1]) / ((degree + 1) * table[:, degree])
    node_points = np.sort(node_points)
    values = legendre_columns(node_points, degree)[:, degree]
    matrix = np.zeros((NP, NP))
    for row_index in range(NP):
        for col_index in range(NP):
            if row_index != col_index:
                matrix[row_index, col_index] = values[row_index] / (values[col_index] * (node_points[row_index] - node_points[col_index]))
    matrix[0, 0] = -degree * (degree + 1) / 4.0
    matrix[-1, -1] = degree * (degree + 1) / 4.0
    return matrix

def schwarz_tables():
    grid_count = NP + 2
    mode_index = np.arange(1, grid_count + 1)
    sine_basis = math.sqrt(2.0 / (grid_count + 1)) * np.sin(np.pi * np.outer(mode_index, mode_index) / (grid_count + 1))
    eigen_values = 2.0 - 2.0 * np.cos(np.pi * mode_index / (grid_count + 1))
    return (sine_basis, eigen_values)

def derive(volume, direction, deriv_scale, diff_table):
    patterns = ('pi,cijke->cpjke', 'pj,cijke->cipke', 'pk,cijke->cijpe')
    result = jnp.einsum(patterns[direction], diff_table, volume, precision=lax.Precision.HIGHEST)
    return result * deriv_scale

def faces_of(volume):
    channels = volume.shape[0]
    elements = volume.shape[-1]
    face_parts = [volume[:, 0], volume[:, -1], volume[:, :, 0], volume[:, :, -1], volume[:, :, :, 0], volume[:, :, :, -1]]
    return [face_piece.reshape(channels, NP * NP, elements) for face_piece in face_parts]

def add_faces(volume, face_terms):
    channels = volume.shape[0]
    elements = volume.shape[-1]
    shaped = [face_piece.reshape(channels, NP, NP, elements) for face_piece in face_terms]
    volume = volume.at[:, 0].add(shaped[0])
    volume = volume.at[:, -1].add(shaped[1])
    volume = volume.at[:, :, 0].add(shaped[2])
    volume = volume.at[:, :, -1].add(shaped[3])
    volume = volume.at[:, :, :, 0].add(shaped[4])
    volume = volume.at[:, :, :, -1].add(shaped[5])
    return volume

def advance(velocity, base_field, base_grads, deriv_scale, diff_table, adjacent):
    own_faces = faces_of(velocity)
    gradients = [derive(velocity, direction, deriv_scale, diff_table) for direction in range(3)]
    transport = sum((base_field[direction] * gradients[direction] for direction in range(3)))
    diffuse = sum((derive(gradients[direction], direction, deriv_scale, diff_table) for direction in range(3)))
    reaction = -jnp.stack([lax.optimization_barrier(jnp.sum(velocity * base_grads[direction], axis=0)) for direction in range(3)])
    updated = velocity + time_step * (transport + reaction + viscosity * diffuse)
    face_terms = [penalty * (adjacent[index] - own_faces[index]) for index in range(6)]
    return add_faces(updated, face_terms)

def divergence(velocity, deriv_scale, diff_table):
    return sum((derive(velocity[direction:direction + 1], direction, deriv_scale, diff_table) for direction in range(3)))

def transform(volume, sine_basis):
    patterns = ('pi,cijke->cpjke', 'pj,cijke->cipke', 'pk,cijke->cijpe')
    for pattern in patterns:
        volume = jnp.einsum(pattern, sine_basis, volume, precision=lax.Precision.HIGHEST)
    return volume

def local_solve(residual, adjacent, deriv_scale, sine_basis, eigen_values):
    channels = residual.shape[0]
    elements = residual.shape[-1]
    extended = jnp.pad(residual, ((0, 0), (1, 1), (1, 1), (1, 1), (0, 0)))
    shaped = [face_piece.reshape(channels, NP, NP, elements) for face_piece in adjacent]
    extended = extended.at[:, 0, 1:-1, 1:-1].set(shaped[0])
    extended = extended.at[:, -1, 1:-1, 1:-1].set(shaped[1])
    extended = extended.at[:, 1:-1, 0, 1:-1].set(shaped[2])
    extended = extended.at[:, 1:-1, -1, 1:-1].set(shaped[3])
    extended = extended.at[:, 1:-1, 1:-1, 0].set(shaped[4])
    extended = extended.at[:, 1:-1, 1:-1, -1].set(shaped[5])
    scale_square = (deriv_scale * 0.5) ** 2
    spectrum = eigen_values[:, None, None] + eigen_values[None, :, None] + eigen_values[None, None, :]
    divisor = spectrum[None, :, :, :, None] * scale_square + shift_term
    forward = transform(extended, sine_basis)
    return transform(forward / divisor, sine_basis)

def outer_layers(solved):
    channels = solved.shape[0]
    elements = solved.shape[-1]
    face_parts = [solved[:, 0, 1:-1, 1:-1], solved[:, -1, 1:-1, 1:-1], solved[:, 1:-1, 0, 1:-1], solved[:, 1:-1, -1, 1:-1], solved[:, 1:-1, 1:-1, 0], solved[:, 1:-1, 1:-1, -1]]
    return [face_piece.reshape(channels, NP * NP, elements) for face_piece in face_parts]

def to_volume(flattened):
    return flattened.reshape(flattened.shape[0], NP, NP, NP, flattened.shape[-1])

def to_blocks(array):
    shaped = array.reshape(array.shape[:-1] + (N_LEAF * N_LOBE, E_DEV))
    return jnp.moveaxis(shaped, -2, 0)

def from_blocks(array):
    moved = jnp.moveaxis(array, 0, -2)
    return moved.reshape(moved.shape[:-2] + (N_LEAF * N_LOBE * E_DEV,))

def reference_near(own_faces, link_slot):
    channels = own_faces[0].shape[0]
    face_width = own_faces[0].shape[1]

    def to_grid(face_array):
        return face_array.reshape(channels, face_width, N_LEAF, N_LOBE, E_DEV)

    def to_chain(face_array):
        return jnp.transpose(to_grid(face_array), (0, 1, 3, 2, 4)).reshape(channels, face_width, N_LOBE, N_LEAF * E_DEV)

    def unchain(face_array):
        shaped = face_array.reshape(channels, face_width, N_LOBE, N_LEAF, E_DEV)
        return jnp.transpose(shaped, (0, 1, 3, 2, 4)).reshape(channels, face_width, -1)
    lead_faces = to_chain(own_faces[0])
    tail_faces = to_chain(own_faces[1])
    zero_column = jnp.zeros_like(lead_faces[..., :1])
    near_zero = unchain(jnp.concatenate([zero_column, tail_faces[..., :-1]], axis=-1))
    near_one = unchain(jnp.concatenate([lead_faces[..., 1:], zero_column], axis=-1))
    lower_faces = to_grid(own_faces[4])
    upper_faces = to_grid(own_faces[5])
    zero_lobe = jnp.zeros_like(lower_faces[:, :, :, :1])
    near_four = jnp.concatenate([zero_lobe, upper_faces[:, :, :, :-1]], axis=3).reshape(channels, face_width, -1)
    near_five = jnp.concatenate([lower_faces[:, :, :, 1:], zero_lobe], axis=3).reshape(channels, face_width, -1)
    side_faces = jnp.concatenate([to_grid(own_faces[2]), to_grid(own_faces[3])], axis=-1)
    flattened = side_faces.reshape(channels, face_width, -1)
    slot_table = link_slot.reshape(N_LEAF, N_LOBE, N_LEAF, CAP)
    partner = jnp.transpose(slot_table, (2, 1, 0, 3))
    leaf_index = jnp.arange(N_LEAF, dtype=jnp.int32).reshape(N_LEAF, 1, 1, 1)
    lobe_index = jnp.arange(N_LOBE, dtype=jnp.int32).reshape(1, N_LOBE, 1, 1)
    peer_index = jnp.arange(N_LEAF, dtype=jnp.int32).reshape(1, 1, N_LEAF, 1)
    is_linked = slot_table >= 0
    source = (peer_index * N_LOBE + lobe_index) * (2 * E_DEV) + partner
    target = (leaf_index * N_LOBE + lobe_index) * (2 * E_DEV) + slot_table
    slot_total = N_LEAF * N_LOBE * 2 * E_DEV
    source = jnp.where(is_linked, source, 0).reshape(-1).astype(jnp.int32)
    target = jnp.where(is_linked, target, slot_total).reshape(-1).astype(jnp.int32)
    values = jnp.take(flattened, source, axis=2)
    gathered = jnp.zeros_like(flattened).at[:, :, target].add(values, mode='drop')
    gathered = gathered.reshape(channels, face_width, N_LEAF, N_LOBE, 2, E_DEV)
    near_two = gathered[:, :, :, :, 0, :].reshape(channels, face_width, -1)
    near_three = gathered[:, :, :, :, 1, :].reshape(channels, face_width, -1)
    return [near_zero, near_one, near_two, near_three, near_four, near_five]

def reference(base_velocity, adjoint_velocity, element_size, link_slot):
    diff_table = jnp.asarray(node_tables(), jnp.float32)
    basis_table, eigen_table = schwarz_tables()
    sine_basis = jnp.asarray(basis_table, jnp.float32)
    eigen_values = jnp.asarray(eigen_table, jnp.float32)
    base_blocks = to_blocks(base_velocity)
    size_blocks = to_blocks(element_size)

    def one_block(operands):
        block_velocity, block_base, block_size, block_near = operands
        deriv_scale = 2.0 / block_size
        base_field = to_volume(block_base)
        base_grads = [derive(base_field, direction, deriv_scale, diff_table) for direction in range(3)]
        moved = advance(to_volume(block_velocity), base_field, base_grads, deriv_scale, diff_table, list(block_near))
        return moved.reshape(block_velocity.shape)
    velocity = adjoint_velocity
    for step_index in range(STEPS):
        adjacent = reference_near(faces_of(to_volume(velocity)), link_slot)
        near_blocks = tuple((to_blocks(face_array) for face_array in adjacent))
        velocity = from_blocks(lax.map(one_block, (to_blocks(velocity), base_blocks, size_blocks, near_blocks)))

    def divergence_block(operands):
        block_velocity, block_size = operands
        return divergence(to_volume(block_velocity), 2.0 / block_size, diff_table).reshape(1, NP * NP * NP, -1)
    residual = from_blocks(lax.map(divergence_block, (to_blocks(velocity), size_blocks)))
    adjacent = reference_near(faces_of(to_volume(residual)), link_slot)

    def solve_block(operands):
        block_residual, block_size, block_near = operands
        solved = local_solve(to_volume(block_residual), list(block_near), 2.0 / block_size, sine_basis, eigen_values)
        interior = solved[:, 1:-1, 1:-1, 1:-1].reshape(block_residual.shape)
        return (interior, tuple(outer_layers(solved)))
    near_blocks = tuple((to_blocks(face_array) for face_array in adjacent))
    interior, outer = lax.map(solve_block, (to_blocks(residual), size_blocks, near_blocks))
    interior = from_blocks(interior)
    outer = [from_blocks(face_array) for face_array in outer]
    returned = reference_near(outer, link_slot)
    pressure = add_faces(to_volume(interior), returned)
    return (velocity, pressure.reshape(NP * NP * NP, -1))
```

```python
import functools
import math

import jax
import jax.numpy as jnp
import numpy as np
from jax import lax
from jax.experimental import pallas as pl
from jax.experimental.pallas import tpu as pltpu
from jax.sharding import PartitionSpec as P

NP = 8
EL = 256
MODES = 104
MODES16 = 112

time_step = 0.01
viscosity = 0.002
penalty = 0.5
shift_term = 1.0

F32 = jnp.float32
BF16 = jnp.bfloat16


def legendre_columns(points, degree):
    table = np.zeros((points.shape[0], degree + 1))
    table[:, 0] = 1.0
    table[:, 1] = points
    for order in range(2, degree + 1):
        table[:, order] = (
            (2 * order - 1) * points * table[:, order - 1] - (order - 1) * table[:, order - 2]
        ) / order
    return table


def node_tables():
    degree = NP - 1
    node_points = np.cos(np.pi * np.arange(degree + 1) / degree)
    for sweep in range(100):
        table = legendre_columns(node_points, degree)
        node_points = node_points - (node_points * table[:, degree] - table[:, degree - 1]) / (
            (degree + 1) * table[:, degree]
        )
    node_points = np.sort(node_points)
    values = legendre_columns(node_points, degree)[:, degree]
    matrix = np.zeros((NP, NP))
    for row_index in range(NP):
        for col_index in range(NP):
            if row_index != col_index:
                matrix[row_index, col_index] = values[row_index] / (
                    values[col_index] * (node_points[row_index] - node_points[col_index])
                )
    matrix[0, 0] = -degree * (degree + 1) / 4.0
    matrix[-1, -1] = degree * (degree + 1) / 4.0
    return matrix


def schwarz_tables():
    grid_count = NP + 2
    mode_index = np.arange(1, grid_count + 1)
    sine_basis = math.sqrt(2.0 / (grid_count + 1)) * np.sin(
        np.pi * np.outer(mode_index, mode_index) / (grid_count + 1)
    )
    eigen_values = 2.0 - 2.0 * np.cos(np.pi * mode_index / (grid_count + 1))
    return (sine_basis, eigen_values)


def three(matrix):
    high = matrix.astype(np.float32).astype(jnp.bfloat16)
    low = (matrix - high.astype(np.float64)).astype(np.float32).astype(jnp.bfloat16)
    return np.concatenate([high, low, high], axis=1)


WIDE = 384
ROW_JK, ROW_IK, ROW_DIV, ROW_INT, ROW_LAY, ROW_BACK, ROW_END = 0, 192, 320, 384, 496, 608, 704


def constant_tables():
    diff = node_tables().astype(np.float32).astype(np.float64)
    sine, eigen = schwarz_tables()
    sine = sine.astype(np.float32).astype(np.float64)
    one = np.eye(NP)
    first, second = np.kron(diff, one), np.kron(one, diff)
    plane = np.concatenate([first, second, first @ first + second @ second], axis=0)
    along = np.concatenate([first, first @ first], axis=0)
    table = np.zeros((ROW_END, WIDE), jnp.bfloat16)
    table[ROW_JK : ROW_JK + 192, :192] = three(plane)
    table[ROW_IK : ROW_IK + 128, :192] = three(along)
    table[ROW_DIV : ROW_DIV + 64, :384] = np.concatenate([three(first), three(second)], axis=1)
    both = np.kron(sine, sine)
    grid = np.arange(100).reshape(10, 10)
    inner = grid[1:9, 1:9].reshape(-1)
    layers = np.concatenate([grid[0, 1:9], grid[9, 1:9], grid[1:9, 0], grid[1:9, 9]])
    forward = np.zeros((MODES16, 100))
    forward[:100] = both
    table[ROW_INT : ROW_INT + MODES16, :192] = three(forward[:, inner])
    table[ROW_LAY : ROW_LAY + MODES16, :96] = three(forward[:, layers])
    backward = np.zeros((96, MODES16))
    backward[:, :100] = both[np.concatenate([inner, layers])]
    table[ROW_BACK : ROW_BACK + 96, : 3 * MODES16] = three(backward)
    sums = np.zeros((MODES,))
    sums[:100] = (eigen[:, None] + eigen[None, :]).reshape(-1)
    sums = np.tile(sums[:, None], (1, 128)).astype(np.float32)
    return table, sums


def split(x):
    high = x.astype(BF16)
    low = (x - high.astype(F32)).astype(BF16)
    return high, low


def stack(x):
    high, low = split(x)
    return jnp.concatenate([high, high, low], axis=0)


def ld(ref, at, size):
    half = ref.shape[0] // 2
    return jnp.concatenate([ref[pl.ds(at, size), :], ref[pl.ds(half + at, size), :]], axis=1)


def st(ref, at, value):
    half, size = ref.shape[0] // 2, value.shape[0]
    ref[pl.ds(at, size), :] = value[:, :128]
    ref[pl.ds(half + at, size), :] = value[:, 128:]


def add(ref, at, value):
    st(ref, at, ld(ref, at, value.shape[0]) + value)


def ends_of(ref, at, k):
    half = ref.shape[0] // 2
    return [pl.ds(h * half + at + k, 64, stride=8) for h in range(2)]


def dot(a, b):
    return lax.dot_general(a, b, (((1,), (0,)), ((), ())), preferred_element_type=F32)


def dot_nt(a, b):
    return lax.dot_general(a, b, (((1,), (1,)), ((), ())), preferred_element_type=F32)


def kernel(
    leaves, lobes,
    base_hbm, adj_hbm, size_hbm, slot_hbm, table_hbm, sums_hbm,
    out_hbm, press_hbm,
    base, v0, v1, v2, grads, part, res, modes, recip, press, outer,
    size, slot, table, sums,
    zs, zr, zs1, zr1, msg, recv, a_lo, a_hi, chain_out, chain_in,
    in_sem, out_sem, z_send, z_recv, l_send, l_recv,
):
    me = lax.axis_index("leaf")
    lobe = lax.axis_index("lobe")
    rows = leaves * 8
    sine, eigen = schwarz_tables()

    loads = [
        pltpu.make_async_copy(slot_hbm, slot, in_sem.at[0]),
        pltpu.make_async_copy(adj_hbm.at[:, 0:128], v0.at[0:1536], in_sem.at[1]),
        pltpu.make_async_copy(table_hbm, table, in_sem.at[2]),
        pltpu.make_async_copy(size_hbm, size, in_sem.at[3]),
        pltpu.make_async_copy(base_hbm, base, in_sem.at[4]),
        pltpu.make_async_copy(sums_hbm, sums, in_sem.at[5]),
        pltpu.make_async_copy(adj_hbm.at[:, 128:256], v0.at[1536:3072], in_sem.at[6]),
    ]
    for load in loads:
        load.start()

    for x in range(4):
        recv[x, pl.ds(pl.multiple_of(me * 8, 8), 8), :] = jnp.zeros((8, 128), F32)

    @pl.when(lobe == 0)
    def _():
        zr[:, 0] = jnp.zeros((2, 192, EL), F32)
        zr1[:, 0] = jnp.zeros((2, 64, EL), F32)

    @pl.when(lobe == lobes - 1)
    def _():
        zr[:, 1] = jnp.zeros((2, 192, EL), F32)
        zr1[:, 1] = jnp.zeros((2, 64, EL), F32)

    barrier = pltpu.get_barrier_semaphore()

    def greet(d, carry):
        pl.semaphore_signal(
            barrier, inc=1, device_id={"leaf": lax.rem(me + d, leaves)},
            device_id_type=pl.DeviceIdType.MESH,
        )
        return carry

    lax.fori_loop(1, leaves, greet, 0)

    @pl.when(lobe > 0)
    def _():
        pl.semaphore_signal(
            barrier, inc=1, device_id={"lobe": lobe - 1}, device_id_type=pl.DeviceIdType.MESH
        )

    @pl.when(lobe < lobes - 1)
    def _():
        pl.semaphore_signal(
            barrier, inc=1, device_id={"lobe": lobe + 1}, device_id_type=pl.DeviceIdType.MESH
        )

    loads[0].wait()
    hot = (lax.broadcasted_iota(jnp.int32, (512, leaves * 4), 0) == slot[...]).astype(F32)
    row = lax.broadcasted_iota(jnp.int32, (rows, leaves * 4), 0)
    col = lax.broadcasted_iota(jnp.int32, (rows, leaves * 4), 1)
    spread = ((row >> 3) * 4 + (row & 3) == col).astype(F32)
    all_hot = dot_nt(spread.astype(BF16), hot.astype(BF16))
    low_row = (lax.broadcasted_iota(jnp.int32, (rows, 512), 0) & 4) == 0
    a_lo[...] = jnp.where(low_row, all_hot, 0.0).astype(BF16)
    a_hi[...] = jnp.where(low_row, 0.0, all_hot).astype(BF16)
    for cc in range(3):
        row = lax.broadcasted_iota(jnp.int32, (rows, 128), 0)
        col = lax.broadcasted_iota(jnp.int32, (rows, 128), 1)
        after, before = (me + 1) * 8 + 4 + cc, (me - 1) * 8 + 4 + cc
        pick = ((row == after) & (col == 127)) | ((row == before) & (col == 0))
        chain_out[:, cc * 128 : cc * 128 + 128] = pick.astype(F32).astype(BF16)
        row = lax.broadcasted_iota(jnp.int32, (rows, EL), 0)
        col = lax.broadcasted_iota(jnp.int32, (rows, EL), 1)
        put = ((row == before) & (col == 0)) | ((row == after) & (col == EL - 1))
        chain_in[:, cc * EL : (cc + 1) * EL] = put.astype(F32).astype(BF16)

    def start_z(sends, recvs, at, x):
        @pl.when(lobe < lobes - 1)
        def _():
            pltpu.make_async_remote_copy(
                sends.at[at, 1], recvs.at[at, 0], z_send.at[x, 1], z_recv.at[x, 0],
                device_id={"lobe": lobe + 1}, device_id_type=pl.DeviceIdType.MESH,
            ).start()

        @pl.when(lobe > 0)
        def _():
            pltpu.make_async_remote_copy(
                sends.at[at, 0], recvs.at[at, 1], z_send.at[x, 0], z_recv.at[x, 1],
                device_id={"lobe": lobe - 1}, device_id_type=pl.DeviceIdType.MESH,
            ).start()

    def wait_z(sends, recvs, at, x, sent):
        @pl.when(lobe < lobes - 1)
        def _():
            copy = pltpu.make_async_remote_copy(
                sends.at[at, 1], recvs.at[at, 1], z_send.at[x, 1], z_recv.at[x, 1],
                device_id={"lobe": lobe + 1}, device_id_type=pl.DeviceIdType.MESH,
            )
            copy.wait_send() if sent else copy.wait_recv()

        @pl.when(lobe > 0)
        def _():
            copy = pltpu.make_async_remote_copy(
                sends.at[at, 0], recvs.at[at, 0], z_send.at[x, 0], z_recv.at[x, 0],
                device_id={"lobe": lobe - 1}, device_id_type=pl.DeviceIdType.MESH,
            )
            copy.wait_send() if sent else copy.wait_recv()

    def start_links(x):
        def body(d, carry):
            peer = lax.rem(me + d, leaves)
            pltpu.make_async_remote_copy(
                msg.at[x, pl.ds(pl.multiple_of(peer * 8, 8), 8)],
                recv.at[x, pl.ds(pl.multiple_of(me * 8, 8), 8)],
                l_send.at[x], l_recv.at[x],
                device_id={"leaf": peer}, device_id_type=pl.DeviceIdType.MESH,
            ).start()
            return carry

        lax.fori_loop(1, leaves, body, 0)

    def wait_links(x, sent):
        copy = pltpu.make_async_remote_copy(
            msg.at[x, pl.ds(0, rows - 8)], recv.at[x, pl.ds(0, rows - 8)],
            l_send.at[x], l_recv.at[x],
            device_id={"leaf": lax.rem(me + 1, leaves)}, device_id_type=pl.DeviceIdType.MESH,
        )
        copy.wait_send() if sent else copy.wait_recv()

    def zeros64(width):
        return jnp.zeros((64, width), F32)

    def fill_message(x, face2, face3, leads, tails):
        count = len(leads)
        total = jnp.zeros((rows, 128), F32)
        lane = lax.broadcasted_iota(jnp.int32, (64, 128), 1)
        for f, face in enumerate((face2, face3)):
            if count == 3:
                for piece in split(face[:128]):
                    total += dot_nt(a_lo[:, f * EL : (f + 1) * EL], piece)
            last = jnp.concatenate([face[-64:], zeros64(EL)], axis=0)
            for piece in split(last):
                total += dot_nt(a_hi[:, f * EL : (f + 1) * EL], piece)
        for cc in range(count):
            ends = jnp.where(lane == 0, leads[cc], jnp.where(lane == 127, tails[cc], 0.0))
            ends = jnp.concatenate([zeros64(128), ends], axis=0)
            for piece in split(ends):
                total += dot_nt(chain_out[:, cc * 128 : (cc + 1) * 128], piece)
        msg[x] = total

    def read_links(x, count):
        turned = jnp.transpose(recv[x])
        high, low = split(turned)
        near = []
        if count == 3:
            near.append(dot(high, a_lo[...]) + dot(low, a_lo[...]))
        near.append((dot(high, a_hi[...]) + dot(low, a_hi[...]))[:64])
        near = jnp.concatenate(near, axis=0) if count == 3 else near[0]
        wide = count * EL
        ends = dot(high[64:], chain_in[:, :wide]) + dot(low[64:], chain_in[:, :wide])
        return near, ends

    def spot(c, i):
        return pl.multiple_of(c * 512 + i * 64, 64)

    def block(c, i):
        return pl.ds(spot(c, i), 64)

    def across(ref, c, j):
        at = [pl.multiple_of(c * 512 + i * 64 + j * 8, 8) for i in range(8)]
        if ref.shape[1] == 128:
            return jnp.concatenate([ld(ref, one, 8) for one in at], axis=0)
        return jnp.concatenate([ref[pl.ds(one, 8), :] for one in at], axis=0)

    def put_across(ref, c, j, value):
        for i in range(8):
            at = pl.multiple_of(c * 512 + i * 64 + j * 8, 8)
            if ref.shape[1] == 128:
                st(ref, at, value[i * 8 : i * 8 + 8])
            else:
                ref[pl.ds(at, 8), :] = value[i * 8 : i * 8 + 8]

    lane = lax.broadcasted_iota(jnp.int32, (64, EL), 1)

    def chain_near(lead, tail):
        near0 = jnp.where(lane == 0, 0.0, pltpu.roll(tail, 1, 1))
        near1 = jnp.where(lane == EL - 1, 0.0, pltpu.roll(lead, EL - 1, 1))
        return near0, near1

    def send_faces(v, x):
        for c in range(3):
            for side, k in ((0, 0), (1, 7)):
                for h, at in enumerate(ends_of(v, c * 512, k)):
                    zs[x, side, c * 64 : c * 64 + 64, h * 128 : h * 128 + 128] = v[at, :]
        if x == 0:
            pl.semaphore_wait(
                barrier,
                leaves - 1 + (lobe > 0).astype(jnp.int32) + (lobe < lobes - 1).astype(jnp.int32),
            )
        start_z(zs, zr, x, x)
        face2 = jnp.concatenate(
            [ld(v, c * 512 + i * 64, 8) for c in range(3) for i in range(8)], axis=0
        )
        face3 = jnp.concatenate(
            [ld(v, c * 512 + i * 64 + 56, 8) for c in range(3) for i in range(8)], axis=0
        )
        leads = [v[c * 512 : c * 512 + 64, :] for c in range(3)]
        tails = [v[1536 + c * 512 + 448 : 1536 + c * 512 + 512, :] for c in range(3)]
        fill_message(x, face2, face3, leads, tails)
        start_links(x)

    def advance(v, w, x):
        scale = 2.0 / size[...]
        visc = viscosity * scale
        step = time_step * scale

        def one(j, carry):
            for c in range(3):
                y = dot(table[ROW_IK : ROW_IK + 128, :192], stack(across(v, c, j)))
                put_across(part, c, j, across(base, 0, j) * y[:64] + visc * y[64:])
            return carry

        lax.fori_loop(0, 8, one, 0, unroll=2)
        sub = lax.broadcasted_iota(jnp.int32, (64, EL), 0)
        k, j = sub & 7, sub >> 3
        edge = ((k == 0) | (k == 7)).astype(F32) + ((j == 0) | (j == 7)).astype(F32)

        def two(i, carry):
            own = [ld(v, spot(r, i), 64) for r in range(3)]
            b1, b2 = base[block(1, i), :], base[block(2, i), :]
            ends = jnp.where((i == 0) | (i == 7), 1.0, 0.0).astype(F32)
            keep = 1.0 - penalty * (edge + ends)
            for c in range(3):
                y = dot(table[ROW_JK : ROW_JK + 192, :192], stack(own[c]))
                total = part[block(c, i), :] + b1 * y[:64] + b2 * y[64:128] + visc * y[128:]
                for r in range(3):
                    total -= own[r] * grads[block(c * 3 + r, i), :]
                st(w, spot(c, i), keep * own[c] + step * total)
            return carry

        lax.fori_loop(0, 8, two, 0, unroll=2)
        for c in range(3):
            near0, near1 = chain_near(ld(v, spot(c, 0), 64), ld(v, spot(c, 7), 64))
            add(w, spot(c, 0), penalty * near0)
            add(w, spot(c, 7), penalty * near1)
        wait_links(x, False)
        near, ends = read_links(x, 3)
        for c in range(3):
            end = ends[:, c * EL : (c + 1) * EL]
            add(w, spot(c, 0), jnp.where(lane == 0, penalty * end, 0.0))
            add(w, spot(c, 7), jnp.where(lane == EL - 1, penalty * end, 0.0))
            for i in range(8):
                for f, j in ((0, 0), (1, 7)):
                    at = c * 512 + i * 64 + j * 8
                    r0 = c * 64 + i * 8
                    add(w, at, penalty * near[r0 : r0 + 8, f * EL : (f + 1) * EL])
        wait_z(zs, zr, x, x, False)
        for c in range(3):
            for side, k in ((0, 0), (1, 7)):
                for h, at in enumerate(ends_of(w, c * 512, k)):
                    near = zr[x, side, c * 64 : c * 64 + 64, h * 128 : h * 128 + 128]
                    w[at, :] = w[at, :] + penalty * near

    loads[1].wait()
    loads[6].wait()
    send_faces(v0, 0)
    loads[2].wait()
    loads[3].wait()
    loads[4].wait()
    loads[5].wait()

    def grad_one(j, carry):
        for r in range(3):
            y = dot(table[ROW_IK : ROW_IK + 64, :192], stack(across(base, r, j)))
            put_across(grads, r, j, y)
        return carry

    lax.fori_loop(0, 8, grad_one, 0, unroll=2)

    def grad_two(i, carry):
        for r in range(3):
            y = dot(table[ROW_JK : ROW_JK + 128, :192], stack(base[block(r, i), :]))
            grads[block(3 + r, i), :] = y[:64]
            grads[block(6 + r, i), :] = y[64:]
        return carry

    lax.fori_loop(0, 8, grad_two, 0, unroll=2)
    advance(v0, v1, 0)

    send_faces(v1, 1)
    scale_square = (1.0 / size[...]) ** 2

    def recip_body(b, carry):
        at = pl.multiple_of(b * 8, 8)
        here = sums[pl.ds(at, 8), :]
        here = jnp.concatenate([here, here], axis=1)
        for m in range(10):
            recip[pl.ds(pl.multiple_of(m * MODES + at, 8), 8), :] = 1.0 / (
                (here + float(eigen[m])) * scale_square + shift_term
            )
        return carry

    lax.fori_loop(0, MODES // 8, recip_body, 0)
    advance(v1, v2, 1)
    out_copies = [
        pltpu.make_async_copy(v2.at[h * 1536 : h * 1536 + 1536], out_hbm.at[:, h * 128 : h * 128 + 128], out_sem.at[h])
        for h in range(2)
    ]
    for copy in out_copies:
        copy.start()

    scale = 2.0 / size[...]

    def div_one(j, carry):
        put_across(res, 0, j, dot(table[ROW_IK : ROW_IK + 64, :192], stack(across(v2, 0, j))))
        return carry

    lax.fori_loop(0, 8, div_one, 0, unroll=4)

    def div_two(i, carry):
        both = jnp.concatenate([stack(ld(v2, spot(1, i), 64)), stack(ld(v2, spot(2, i), 64))], axis=0)
        y = dot(table[ROW_DIV : ROW_DIV + 64, :], both)
        st(res, spot(0, i), scale * (ld(res, spot(0, i), 64) + y))
        return carry

    lax.fori_loop(0, 8, div_two, 0, unroll=4)
    for side, k in ((0, 0), (1, 7)):
        for h, at in enumerate(ends_of(res, 0, k)):
            zs1[0, side, :, h * 128 : h * 128 + 128] = res[at, :]
    start_z(zs1, zr1, 0, 2)
    face2 = jnp.concatenate([ld(res, i * 64, 8) for i in range(8)], axis=0)
    face3 = jnp.concatenate([ld(res, i * 64 + 56, 8) for i in range(8)], axis=0)
    fill_message(2, face2, face3, [res[0:64, :]], [res[512 + 448 : 512 + 512, :]])
    start_links(2)

    def forward(i, carry):
        y = dot(table[ROW_INT : ROW_INT + MODES16, :192], stack(ld(res, spot(0, i), 64)))
        modes[pl.ds(pl.multiple_of((i + 1) * MODES, 8), MODES), :] = y[:MODES]
        return carry

    lax.fori_loop(0, 8, forward, 0, unroll=4)
    near0, near1 = chain_near(ld(res, 0, 64), ld(res, 448, 64))
    wait_links(2, False)
    near, ends = read_links(2, 1)
    near0 = jnp.where(lane == 0, ends, near0)
    near1 = jnp.where(lane == EL - 1, ends, near1)
    for n, plane in ((0, near0), (9, near1)):
        y = dot(table[ROW_INT : ROW_INT + MODES16, :192], stack(plane))
        modes[n * MODES : (n + 1) * MODES, :] = y[:MODES]
    wait_z(zs1, zr1, 0, 2, False)
    for i in range(8):
        r0 = slice(i * 8, i * 8 + 8)
        layer = jnp.concatenate(
            [near[r0, :EL], near[r0, EL:], zr1[0, 0, r0, :], zr1[0, 1, r0, :]], axis=0
        )
        y = dot(table[ROW_LAY : ROW_LAY + MODES16, :96], stack(layer))
        modes[(i + 1) * MODES : (i + 2) * MODES, :] += y[:MODES]

    def along(values):
        plus = [values[n] + values[9 - n] for n in range(5)]
        minus = [values[n] - values[9 - n] for n in range(5)]
        result = []
        for m in range(10):
            terms = plus if m % 2 == 0 else minus
            total = terms[0] * float(np.float32(sine[m, 0]))
            for n in range(1, 5):
                total += terms[n] * float(np.float32(sine[m, n]))
            result.append(total)
        return result

    def solve(b, carry):
        at = [pl.ds(pl.multiple_of(m * MODES + b * 8, 8), 8) for m in range(10)]
        values = along([modes[at[m], :] for m in range(10)])
        values = along([values[m] * recip[at[m], :] for m in range(10)])
        for m in range(10):
            modes[at[m], :] = values[m]
        return carry

    lax.fori_loop(0, MODES // 8, solve, 0)

    pad = jnp.zeros((MODES16 - MODES, EL), F32)
    for n, at in ((0, 0), (9, 64)):
        plane = jnp.concatenate([modes[n * MODES : (n + 1) * MODES, :], pad], axis=0)
        outer[at : at + 64, :] = dot(table[ROW_BACK : ROW_BACK + 64, : 3 * MODES16], stack(plane))

    def backward(i, carry):
        plane = modes[pl.ds(pl.multiple_of((i + 1) * MODES, 8), MODES), :]
        plane = jnp.concatenate([plane, pad], axis=0)
        y = dot(table[ROW_BACK : ROW_BACK + 96, : 3 * MODES16], stack(plane))
        st(press, spot(0, i), y[:64])
        r0 = pl.multiple_of(i * 8, 8)
        outer[pl.ds(128 + r0, 8), :] = y[64:72]
        outer[pl.ds(192 + r0, 8), :] = y[72:80]
        zs1[1, 0, pl.ds(r0, 8), :] = y[80:88]
        zs1[1, 1, pl.ds(r0, 8), :] = y[88:96]
        return carry

    lax.fori_loop(0, 8, backward, 0, unroll=4)
    start_z(zs1, zr1, 1, 3)
    fill_message(
        3, outer[128:192, :], outer[192:256, :], [outer[0:64, 0:128]], [outer[64:128, 128:256]]
    )
    start_links(3)
    near0, near1 = chain_near(outer[0:64, :], outer[64:128, :])
    wait_links(3, False)
    near, ends = read_links(3, 1)
    add(press, 0, jnp.where(lane == 0, ends, near0))
    add(press, 448, jnp.where(lane == EL - 1, ends, near1))
    for i in range(8):
        for f, j in ((0, 0), (1, 7)):
            at = i * 64 + j * 8
            add(press, at, near[i * 8 : i * 8 + 8, f * EL : (f + 1) * EL])
    wait_z(zs1, zr1, 1, 3, False)
    for side, k in ((0, 0), (1, 7)):
        for h, at in enumerate(ends_of(press, 0, k)):
            press[at, :] = press[at, :] + zr1[1, side, :, h * 128 : h * 128 + 128]
    press_copies = [
        pltpu.make_async_copy(press.at[h * 512 : h * 512 + 512], press_hbm.at[:, h * 128 : h * 128 + 128], out_sem.at[2 + h])
        for h in range(2)
    ]
    for copy in press_copies:
        copy.start()
    for x in range(4):
        wait_links(x, True)
        if x < 2:
            wait_z(zs, zr, x, x, True)
        else:
            wait_z(zs1, zr1, x - 2, x, True)
    for copy in out_copies + press_copies:
        copy.wait()


def local(leaves, lobes, base_velocity, adjoint_velocity, element_size, link_slot):
    table, sums = constant_tables()
    rows = leaves * 8
    any_space = pl.BlockSpec(memory_space=pl.ANY)
    scratch = [
        pltpu.VMEM((1536, EL), F32),
        pltpu.VMEM((3072, 128), F32),
        pltpu.VMEM((3072, 128), F32),
        pltpu.VMEM((3072, 128), F32),
        pltpu.VMEM((9 * 512, EL), F32),
        pltpu.VMEM((1536, EL), F32),
        pltpu.VMEM((1024, 128), F32),
        pltpu.VMEM((10 * MODES, EL), F32),
        pltpu.VMEM((10 * MODES, EL), F32),
        pltpu.VMEM((1024, 128), F32),
        pltpu.VMEM((256, EL), F32),
        pltpu.VMEM((1, EL), F32),
        pltpu.VMEM((1, leaves * 4), jnp.int32),
        pltpu.VMEM((ROW_END, WIDE), BF16),
        pltpu.VMEM((MODES, 128), F32),
        pltpu.VMEM((2, 2, 192, EL), F32),
        pltpu.VMEM((2, 2, 192, EL), F32),
        pltpu.VMEM((2, 2, 64, EL), F32),
        pltpu.VMEM((2, 2, 64, EL), F32),
        pltpu.VMEM((4, rows, 128), F32),
        pltpu.VMEM((4, rows, 128), F32),
        pltpu.VMEM((rows, 512), BF16),
        pltpu.VMEM((rows, 512), BF16),
        pltpu.VMEM((rows, 384), BF16),
        pltpu.VMEM((rows, 768), BF16),
        pltpu.SemaphoreType.DMA((7,)),
        pltpu.SemaphoreType.DMA((4,)),
        pltpu.SemaphoreType.DMA((4, 2)),
        pltpu.SemaphoreType.DMA((4, 2)),
        pltpu.SemaphoreType.DMA((4,)),
        pltpu.SemaphoreType.DMA((4,)),
    ]
    out, press = pl.pallas_call(
        functools.partial(kernel, leaves, lobes),
        out_shape=(
            jax.ShapeDtypeStruct((1536, EL), F32),
            jax.ShapeDtypeStruct((512, EL), F32),
        ),
        in_specs=[any_space] * 6,
        out_specs=(any_space, any_space),
        scratch_shapes=scratch,
        compiler_params=pltpu.CompilerParams(
            collective_id=0, has_side_effects=True, vmem_limit_bytes=40 * 1024 * 1024
        ),
    )(
        base_velocity.reshape(1536, EL),
        adjoint_velocity.reshape(1536, EL),
        element_size.reshape(1, EL),
        link_slot.reshape(1, leaves * 4),
        jnp.asarray(table),
        jnp.asarray(sums),
    )
    return out.reshape(3, 512, EL), press


def solution(mesh):
    placed = (
        P(None, None, ("leaf", "lobe")),
        P(None, None, ("leaf", "lobe")),
        P(("leaf", "lobe")),
        P(("leaf", "lobe")),
    )
    return jax.shard_map(
        functools.partial(local, mesh.shape["leaf"], mesh.shape["lobe"]),
        mesh=mesh,
        in_specs=placed,
        out_specs=(P(None, None, ("leaf", "lobe")), P(None, ("leaf", "lobe"))),
        check_vma=False,
    )
```

```python
import functools
import math

import jax
import jax.numpy as jnp
import numpy as np
from jax import lax
from jax.experimental import pallas as pl
from jax.experimental.pallas import tpu as pltpu
from jax.sharding import PartitionSpec as P

NP = 8
PIECES = 3
EL = 256
MODES = 104
MODES16 = 112

time_step = 0.01
viscosity = 0.002
penalty = 0.5
shift_term = 1.0

F32 = jnp.float32
BF16 = jnp.bfloat16


def legendre_columns(points, degree):
    table = np.zeros((points.shape[0], degree + 1))
    table[:, 0] = 1.0
    table[:, 1] = points
    for order in range(2, degree + 1):
        table[:, order] = (
            (2 * order - 1) * points * table[:, order - 1] - (order - 1) * table[:, order - 2]
        ) / order
    return table


def node_tables():
    degree = NP - 1
    node_points = np.cos(np.pi * np.arange(degree + 1) / degree)
    for sweep in range(100):
        table = legendre_columns(node_points, degree)
        node_points = node_points - (node_points * table[:, degree] - table[:, degree - 1]) / (
            (degree + 1) * table[:, degree]
        )
    node_points = np.sort(node_points)
    values = legendre_columns(node_points, degree)[:, degree]
    matrix = np.zeros((NP, NP))
    for row_index in range(NP):
        for col_index in range(NP):
            if row_index != col_index:
                matrix[row_index, col_index] = values[row_index] / (
                    values[col_index] * (node_points[row_index] - node_points[col_index])
                )
    matrix[0, 0] = -degree * (degree + 1) / 4.0
    matrix[-1, -1] = degree * (degree + 1) / 4.0
    return matrix


def schwarz_tables():
    grid_count = NP + 2
    mode_index = np.arange(1, grid_count + 1)
    sine_basis = math.sqrt(2.0 / (grid_count + 1)) * np.sin(
        np.pi * np.outer(mode_index, mode_index) / (grid_count + 1)
    )
    eigen_values = 2.0 - 2.0 * np.cos(np.pi * mode_index / (grid_count + 1))
    return (sine_basis, eigen_values)


def three(matrix):
    high = matrix.astype(np.float32).astype(jnp.bfloat16)
    low = (matrix - high.astype(np.float64)).astype(np.float32).astype(jnp.bfloat16)
    return np.concatenate([high, low, high], axis=1)


WIDE = 384
ROW_JK, ROW_IK, ROW_DIV, ROW_INT, ROW_LAY, ROW_BACK, ROW_END = 0, 192, 320, 384, 496, 608, 704


def constant_tables():
    diff = node_tables().astype(np.float32).astype(np.float64)
    sine, eigen = schwarz_tables()
    sine = sine.astype(np.float32).astype(np.float64)
    one = np.eye(NP)
    first, second = np.kron(diff, one), np.kron(one, diff)
    plane = np.concatenate([first, second, first @ first + second @ second], axis=0)
    along = np.concatenate([first, first @ first], axis=0)
    table = np.zeros((ROW_END, WIDE), jnp.bfloat16)
    table[ROW_JK : ROW_JK + 192, :192] = three(plane)
    table[ROW_IK : ROW_IK + 128, :192] = three(along)
    table[ROW_DIV : ROW_DIV + 64, :384] = np.concatenate([three(first), three(second)], axis=1)
    both = np.kron(sine, sine)
    grid = np.arange(100).reshape(10, 10)
    inner = grid[1:9, 1:9].reshape(-1)
    layers = np.concatenate([grid[0, 1:9], grid[9, 1:9], grid[1:9, 0], grid[1:9, 9]])
    forward = np.zeros((MODES16, 100))
    forward[:100] = both
    table[ROW_INT : ROW_INT + MODES16, :192] = three(forward[:, inner])
    table[ROW_LAY : ROW_LAY + MODES16, :96] = three(forward[:, layers])
    backward = np.zeros((96, MODES16))
    backward[:, :100] = both[np.concatenate([inner, layers])]
    table[ROW_BACK : ROW_BACK + 96, : 3 * MODES16] = three(backward)
    sums = np.zeros((MODES,))
    sums[:100] = (eigen[:, None] + eigen[None, :]).reshape(-1)
    sums = np.tile(sums[:, None], (1, 128)).astype(np.float32)
    return table, sums


def split(x):
    high = x.astype(BF16)
    low = (x - high.astype(F32)).astype(BF16)
    return high, low


def stack(x):
    high, low = split(x)
    return jnp.concatenate([high, high, low], axis=0)


def ld(ref, at, size):
    half = ref.shape[0] // 2
    return jnp.concatenate([ref[pl.ds(at, size), :], ref[pl.ds(half + at, size), :]], axis=1)


def st(ref, at, value):
    half, size = ref.shape[0] // 2, value.shape[0]
    ref[pl.ds(at, size), :] = value[:, :128]
    ref[pl.ds(half + at, size), :] = value[:, 128:]


def add(ref, at, value):
    st(ref, at, ld(ref, at, value.shape[0]) + value)


def ends_of(ref, at, k):
    half = ref.shape[0] // 2
    return [pl.ds(h * half + at + k, 64, stride=8) for h in range(2)]


def dot(a, b):
    return lax.dot_general(a, b, (((1,), (0,)), ((), ())), preferred_element_type=F32)


def dot_nt(a, b):
    return lax.dot_general(a, b, (((1,), (1,)), ((), ())), preferred_element_type=F32)


def far_first(me, leaves):
    if leaves != 32:
        return [lax.rem(me + d, leaves) for d in range(1, leaves)]
    hops = [0, 1, 2, 1]
    steps = [(dy, dx, dc) for dy in range(4) for dx in range(4) for dc in range(2)][1:]
    steps.sort(key=lambda one: -(hops[one[0]] + hops[one[1]]))
    y, x, core = me // 8, lax.rem(me // 2, 4), lax.rem(me, 2)
    return [
        lax.rem(y + dy, 4) * 8 + lax.rem(x + dx, 4) * 2 + lax.rem(core + dc, 2)
        for dy, dx, dc in steps
    ]


def kernel(
    leaves, lobes,
    base_hbm, adj_hbm, size_hbm, slot_hbm, table_hbm, sums_hbm,
    out_hbm, press_hbm,
    base, v0, v1, v2, grads, part, res, modes, recip, press, outer,
    size, slot, table, sums,
    zs, zr, zs1, zr1, msg, recv, a_lo, a_hi, chain_out, chain_in,
    in_sem, out_sem, z_send, z_recv, l_send, l_recv,
):
    me = lax.axis_index("leaf")
    lobe = lax.axis_index("lobe")
    rows = leaves * 8
    sine, eigen = schwarz_tables()

    barrier = pltpu.get_barrier_semaphore()
    peers = far_first(me, leaves)
    for peer in peers:
        pl.semaphore_signal(
            barrier, inc=1, device_id={"leaf": peer}, device_id_type=pl.DeviceIdType.MESH
        )

    @pl.when(lobe > 0)
    def _():
        pl.semaphore_signal(
            barrier, inc=1, device_id={"lobe": lobe - 1}, device_id_type=pl.DeviceIdType.MESH
        )

    @pl.when(lobe < lobes - 1)
    def _():
        pl.semaphore_signal(
            barrier, inc=1, device_id={"lobe": lobe + 1}, device_id_type=pl.DeviceIdType.MESH
        )

    loads = [
        pltpu.make_async_copy(slot_hbm, slot, in_sem.at[0]),
        pltpu.make_async_copy(adj_hbm.at[:, 0:128], v0.at[0:1536], in_sem.at[1]),
        pltpu.make_async_copy(table_hbm, table, in_sem.at[2]),
        pltpu.make_async_copy(size_hbm, size, in_sem.at[3]),
        pltpu.make_async_copy(base_hbm, base, in_sem.at[4]),
        pltpu.make_async_copy(sums_hbm, sums, in_sem.at[5]),
        pltpu.make_async_copy(adj_hbm.at[:, 128:256], v0.at[1536:3072], in_sem.at[6]),
    ]
    for load in loads:
        load.start()

    for x in range(4):
        recv[x, pl.ds(pl.multiple_of(me * 8, 8), 8), :] = jnp.zeros((8, 128), F32)

    @pl.when(lobe == 0)
    def _():
        zr[:, 0] = jnp.zeros((2, 192, EL), F32)
        zr1[:, 0] = jnp.zeros((2, 64, EL), F32)

    @pl.when(lobe == lobes - 1)
    def _():
        zr[:, 1] = jnp.zeros((2, 192, EL), F32)
        zr1[:, 1] = jnp.zeros((2, 64, EL), F32)

    loads[0].wait()
    hot = (lax.broadcasted_iota(jnp.int32, (512, leaves * 4), 0) == slot[...]).astype(F32)
    row = lax.broadcasted_iota(jnp.int32, (rows, leaves * 4), 0)
    col = lax.broadcasted_iota(jnp.int32, (rows, leaves * 4), 1)
    spread = ((row >> 3) * 4 + (row & 3) == col).astype(F32)
    all_hot = dot_nt(spread.astype(BF16), hot.astype(BF16))
    low_row = (lax.broadcasted_iota(jnp.int32, (rows, 512), 0) & 4) == 0
    a_lo[...] = jnp.where(low_row, all_hot, 0.0).astype(BF16)
    a_hi[...] = jnp.where(low_row, 0.0, all_hot).astype(BF16)
    for cc in range(3):
        row = lax.broadcasted_iota(jnp.int32, (rows, 128), 0)
        col = lax.broadcasted_iota(jnp.int32, (rows, 128), 1)
        after, before = (me + 1) * 8 + 4 + cc, (me - 1) * 8 + 4 + cc
        pick = ((row == after) & (col == 127)) | ((row == before) & (col == 0))
        chain_out[:, cc * 128 : cc * 128 + 128] = pick.astype(F32).astype(BF16)
        row = lax.broadcasted_iota(jnp.int32, (rows, EL), 0)
        col = lax.broadcasted_iota(jnp.int32, (rows, EL), 1)
        put = ((row == before) & (col == 0)) | ((row == after) & (col == EL - 1))
        chain_in[:, cc * EL : (cc + 1) * EL] = put.astype(F32).astype(BF16)

    def z_copies(sends, recvs, at, x, c):
        rows_of = pl.ds(c * 64, 64)
        up = pltpu.make_async_remote_copy(
            sends.at[at, 1, rows_of], recvs.at[at, 0, rows_of],
            z_send.at[x, 1, c], z_recv.at[x, 0, c],
            device_id={"lobe": lobe + 1}, device_id_type=pl.DeviceIdType.MESH,
        )
        down = pltpu.make_async_remote_copy(
            sends.at[at, 0, rows_of], recvs.at[at, 1, rows_of],
            z_send.at[x, 0, c], z_recv.at[x, 1, c],
            device_id={"lobe": lobe - 1}, device_id_type=pl.DeviceIdType.MESH,
        )
        return up, down

    def start_z(sends, recvs, at, x, c):
        up, down = z_copies(sends, recvs, at, x, c)

        @pl.when(lobe < lobes - 1)
        def _():
            up.start()

        @pl.when(lobe > 0)
        def _():
            down.start()

    def wait_z(sends, recvs, at, x, c, sent):
        up, down = z_copies(sends, recvs, at, x, c)

        @pl.when(lobe < lobes - 1)
        def _():
            up.wait_send() if sent else down.wait_recv()

        @pl.when(lobe > 0)
        def _():
            down.wait_send() if sent else up.wait_recv()

    def start_links(x):
        for peer in peers:
            pltpu.make_async_remote_copy(
                msg.at[x, pl.ds(pl.multiple_of(peer * 8, 8), 8)],
                recv.at[x, pl.ds(pl.multiple_of(me * 8, 8), 8)],
                l_send.at[x], l_recv.at[x],
                device_id={"leaf": peer}, device_id_type=pl.DeviceIdType.MESH,
            ).start()

    def wait_links(x, sent):
        copy = pltpu.make_async_remote_copy(
            msg.at[x, pl.ds(0, rows - 8)], recv.at[x, pl.ds(0, rows - 8)],
            l_send.at[x], l_recv.at[x],
            device_id={"leaf": lax.rem(me + 1, leaves)}, device_id_type=pl.DeviceIdType.MESH,
        )
        copy.wait_send() if sent else copy.wait_recv()

    def zeros64(width):
        return jnp.zeros((64, width), F32)

    def low_message(face2, face3):
        total = jnp.zeros((rows, 128), F32)
        for f, face in enumerate((face2, face3)):
            for piece in split(face):
                total += dot_nt(a_lo[:, f * EL : (f + 1) * EL], piece)
        return total

    def fill_message(x, total, face2, face3, leads, tails):
        end_lane = lax.broadcasted_iota(jnp.int32, (64, 128), 1)
        for f, face in enumerate((face2, face3)):
            for piece in split(jnp.concatenate([face, zeros64(EL)], axis=0)):
                total += dot_nt(a_hi[:, f * EL : (f + 1) * EL], piece)
        for cc in range(len(leads)):
            ends = jnp.where(
                end_lane == 0, leads[cc], jnp.where(end_lane == 127, tails[cc], 0.0)
            )
            ends = jnp.concatenate([zeros64(128), ends], axis=0)
            for piece in split(ends):
                total += dot_nt(chain_out[:, cc * 128 : (cc + 1) * 128], piece)
        msg[x] = total

    def read_links(x, count):
        turned = jnp.transpose(recv[x])
        high, low = split(turned)
        near = []
        if count == 3:
            near.append(dot(high, a_lo[...]) + dot(low, a_lo[...]))
        near.append((dot(high, a_hi[...]) + dot(low, a_hi[...]))[:64])
        near = jnp.concatenate(near, axis=0) if count == 3 else near[0]
        wide = count * EL
        ends = dot(high[64:], chain_in[:, :wide]) + dot(low[64:], chain_in[:, :wide])
        return near, ends

    def spot(c, i):
        return pl.multiple_of(c * 512 + i * 64, 64)

    def block(c, i):
        return pl.ds(spot(c, i), 64)

    def across(ref, c, j):
        at = [pl.multiple_of(c * 512 + i * 64 + j * 8, 8) for i in range(8)]
        if ref.shape[1] == 128:
            return jnp.concatenate([ld(ref, one, 8) for one in at], axis=0)
        return jnp.concatenate([ref[pl.ds(one, 8), :] for one in at], axis=0)

    def put_across(ref, c, j, value):
        for i in range(8):
            at = pl.multiple_of(c * 512 + i * 64 + j * 8, 8)
            if ref.shape[1] == 128:
                st(ref, at, value[i * 8 : i * 8 + 8])
            else:
                ref[pl.ds(at, 8), :] = value[i * 8 : i * 8 + 8]

    lane = lax.broadcasted_iota(jnp.int32, (64, EL), 1)

    def chain_near(lead, tail):
        near0 = jnp.where(lane == 0, 0.0, pltpu.roll(tail, 1, 1))
        near1 = jnp.where(lane == EL - 1, 0.0, pltpu.roll(lead, EL - 1, 1))
        return near0, near1

    def side(v, parts, j):
        return jnp.concatenate(
            [ld(v, c * 512 + i * 64 + j * 8, 8) for c in parts for i in range(8)], axis=0
        )

    def low_faces(v):
        return low_message(side(v, (0, 1), 0), side(v, (0, 1), 7))

    def send_links(v, x, total):
        leads = [v[c * 512 : c * 512 + 64, :] for c in range(3)]
        tails = [v[1536 + c * 512 + 448 : 1536 + c * 512 + 512, :] for c in range(3)]
        fill_message(x, total, side(v, (2,), 0), side(v, (2,), 7), leads, tails)
        start_links(x)

    def advance(v, w, x):
        scale = 2.0 / size[...]
        visc = viscosity * scale
        step = time_step * scale

        def one(j, carry):
            for c in range(3):
                y = dot(table[ROW_IK : ROW_IK + 128, :192], stack(across(v, c, j)))
                put_across(part, c, j, across(base, 0, j) * y[:64] + visc * y[64:])
            return carry

        lax.fori_loop(0, 8, one, 0, unroll=2)
        sub = lax.broadcasted_iota(jnp.int32, (64, EL), 0)
        k, j = sub & 7, sub >> 3
        edge = ((k == 0) | (k == 7)).astype(F32) + ((j == 0) | (j == 7)).astype(F32)

        def two(i, carry):
            own = [ld(v, spot(r, i), 64) for r in range(3)]
            b1, b2 = base[block(1, i), :], base[block(2, i), :]
            ends = jnp.where((i == 0) | (i == 7), 1.0, 0.0).astype(F32)
            keep = 1.0 - penalty * (edge + ends)
            for c in range(3):
                y = dot(table[ROW_JK : ROW_JK + 192, :192], stack(own[c]))
                total = part[block(c, i), :] + b1 * y[:64] + b2 * y[64:128] + visc * y[128:]
                for r in range(3):
                    total -= own[r] * grads[block(c * 3 + r, i), :]
                st(w, spot(c, i), keep * own[c] + step * total)
            return carry

        lax.fori_loop(0, 8, two, 0, unroll=2)
        for c in range(3):
            near0, near1 = chain_near(ld(v, spot(c, 0), 64), ld(v, spot(c, 7), 64))
            add(w, spot(c, 0), penalty * near0)
            add(w, spot(c, 7), penalty * near1)
        wait_links(x, False)
        near, ends = read_links(x, 3)
        for c in range(3):
            end = ends[:, c * EL : (c + 1) * EL]
            add(w, spot(c, 0), jnp.where(lane == 0, penalty * end, 0.0))
            add(w, spot(c, 7), jnp.where(lane == EL - 1, penalty * end, 0.0))
            for i in range(8):
                for f, j in ((0, 0), (1, 7)):
                    at = c * 512 + i * 64 + j * 8
                    r0 = c * 64 + i * 8
                    add(w, at, penalty * near[r0 : r0 + 8, f * EL : (f + 1) * EL])
        total = None
        for c in range(3):
            wait_z(zs, zr, x, x, c, False)
            for f, k in ((0, 0), (1, 7)):
                for h, at in enumerate(ends_of(w, c * 512, k)):
                    here = slice(c * 64, c * 64 + 64), slice(h * 128, h * 128 + 128)
                    value = w[at, :] + penalty * zr[x, f, here[0], here[1]]
                    w[at, :] = value
                    if x == 0:
                        zs[1, f, here[0], here[1]] = value
            if x == 0:
                start_z(zs, zr, 1, 1, c)
                if c == 1:
                    total = low_faces(w)
        if x == 0:
            send_links(w, 1, total)

    loads[1].wait()
    loads[6].wait()
    for c in range(3):
        for f, k in ((0, 0), (1, 7)):
            for h, at in enumerate(ends_of(v0, c * 512, k)):
                zs[0, f, c * 64 : c * 64 + 64, h * 128 : h * 128 + 128] = v0[at, :]
        if c == 0:
            pl.semaphore_wait(
                barrier,
                leaves - 1 + (lobe > 0).astype(jnp.int32) + (lobe < lobes - 1).astype(jnp.int32),
            )
        start_z(zs, zr, 0, 0, c)
    send_links(v0, 0, low_faces(v0))
    loads[2].wait()
    loads[3].wait()
    loads[4].wait()
    loads[5].wait()

    def grad_one(j, carry):
        for r in range(3):
            y = dot(table[ROW_IK : ROW_IK + 64, :192], stack(across(base, r, j)))
            put_across(grads, r, j, y)
        return carry

    lax.fori_loop(0, 8, grad_one, 0, unroll=2)

    def grad_two(i, carry):
        for r in range(3):
            y = dot(table[ROW_JK : ROW_JK + 128, :192], stack(base[block(r, i), :]))
            grads[block(3 + r, i), :] = y[:64]
            grads[block(6 + r, i), :] = y[64:]
        return carry

    lax.fori_loop(0, 8, grad_two, 0, unroll=2)
    advance(v0, v1, 0)

    scale_square = (1.0 / size[...]) ** 2

    def recip_body(b, carry):
        at = pl.multiple_of(b * 8, 8)
        here = sums[pl.ds(at, 8), :]
        here = jnp.concatenate([here, here], axis=1)
        for m in range(10):
            recip[pl.ds(pl.multiple_of(m * MODES + at, 8), 8), :] = 1.0 / (
                (here + float(eigen[m])) * scale_square + shift_term
            )
        return carry

    lax.fori_loop(0, MODES // 8, recip_body, 0)
    advance(v1, v2, 1)
    out_copies = [
        pltpu.make_async_copy(v2.at[h * 1536 : h * 1536 + 1536], out_hbm.at[:, h * 128 : h * 128 + 128], out_sem.at[h])
        for h in range(2)
    ]
    for copy in out_copies:
        copy.start()

    scale = 2.0 / size[...]

    def div_one(j, carry):
        put_across(res, 0, j, dot(table[ROW_IK : ROW_IK + 64, :192], stack(across(v2, 0, j))))
        return carry

    lax.fori_loop(0, 8, div_one, 0, unroll=8)

    def div_two(i, carry):
        both = jnp.concatenate([stack(ld(v2, spot(1, i), 64)), stack(ld(v2, spot(2, i), 64))], axis=0)
        y = dot(table[ROW_DIV : ROW_DIV + 64, :], both)
        st(res, spot(0, i), scale * (ld(res, spot(0, i), 64) + y))
        return carry

    lax.fori_loop(0, 8, div_two, 0, unroll=8)
    face2 = jnp.concatenate([ld(res, i * 64, 8) for i in range(8)], axis=0)
    face3 = jnp.concatenate([ld(res, i * 64 + 56, 8) for i in range(8)], axis=0)
    nothing = jnp.zeros((rows, 128), F32)
    fill_message(2, nothing, face2, face3, [res[0:64, :]], [res[512 + 448 : 512 + 512, :]])
    start_links(2)
    for f, k in ((0, 0), (1, 7)):
        for h, at in enumerate(ends_of(res, 0, k)):
            zs1[0, f, :, h * 128 : h * 128 + 128] = res[at, :]
    start_z(zs1, zr1, 0, 2, 0)

    def forward(i, carry):
        y = dot(table[ROW_INT : ROW_INT + MODES16, :192], stack(ld(res, spot(0, i), 64)))
        modes[pl.ds(pl.multiple_of((i + 1) * MODES, 8), MODES), :] = y[:MODES]
        return carry

    lax.fori_loop(0, 8, forward, 0, unroll=4)
    near0, near1 = chain_near(ld(res, 0, 64), ld(res, 448, 64))
    wait_links(2, False)
    near, ends = read_links(2, 1)
    near0 = jnp.where(lane == 0, ends, near0)
    near1 = jnp.where(lane == EL - 1, ends, near1)
    for n, plane in ((0, near0), (9, near1)):
        y = dot(table[ROW_INT : ROW_INT + MODES16, :192], stack(plane))
        modes[n * MODES : (n + 1) * MODES, :] = y[:MODES]
    wait_z(zs1, zr1, 0, 2, 0, False)
    for i in range(8):
        r0 = slice(i * 8, i * 8 + 8)
        layer = jnp.concatenate(
            [near[r0, :EL], near[r0, EL:], zr1[0, 0, r0, :], zr1[0, 1, r0, :]], axis=0
        )
        y = dot(table[ROW_LAY : ROW_LAY + MODES16, :96], stack(layer))
        modes[(i + 1) * MODES : (i + 2) * MODES, :] += y[:MODES]

    def along(values):
        plus = [values[n] + values[9 - n] for n in range(5)]
        minus = [values[n] - values[9 - n] for n in range(5)]
        result = []
        for m in range(10):
            terms = plus if m % 2 == 0 else minus
            total = terms[0] * float(np.float32(sine[m, 0]))
            for n in range(1, 5):
                total += terms[n] * float(np.float32(sine[m, n]))
            result.append(total)
        return result

    def solve(b, carry):
        at = [pl.ds(pl.multiple_of(m * MODES + b * 8, 8), 8) for m in range(10)]
        values = along([modes[at[m], :] for m in range(10)])
        values = along([values[m] * recip[at[m], :] for m in range(10)])
        for m in range(10):
            modes[at[m], :] = values[m]
        return carry

    lax.fori_loop(0, MODES // 8, solve, 0)

    pad = jnp.zeros((MODES16 - MODES, EL), F32)
    for n, at in ((0, 0), (9, 64)):
        plane = jnp.concatenate([modes[n * MODES : (n + 1) * MODES, :], pad], axis=0)
        outer[at : at + 64, :] = dot(table[ROW_BACK : ROW_BACK + 64, : 3 * MODES16], stack(plane))

    def backward(i, carry):
        plane = modes[pl.ds(pl.multiple_of((i + 1) * MODES, 8), MODES), :]
        plane = jnp.concatenate([plane, pad], axis=0)
        y = dot(table[ROW_BACK : ROW_BACK + 96, : 3 * MODES16], stack(plane))
        st(press, spot(0, i), y[:64])
        r0 = pl.multiple_of(i * 8, 8)
        outer[pl.ds(128 + r0, 8), :] = y[64:72]
        outer[pl.ds(192 + r0, 8), :] = y[72:80]
        zs1[1, 0, pl.ds(r0, 8), :] = y[80:88]
        zs1[1, 1, pl.ds(r0, 8), :] = y[88:96]
        return carry

    lax.fori_loop(0, 8, backward, 0, unroll=8)
    fill_message(
        3, nothing, outer[128:192, :], outer[192:256, :],
        [outer[0:64, 0:128]], [outer[64:128, 128:256]],
    )
    start_links(3)
    start_z(zs1, zr1, 1, 3, 0)
    near0, near1 = chain_near(outer[0:64, :], outer[64:128, :])
    wait_links(3, False)
    near, ends = read_links(3, 1)
    add(press, 0, jnp.where(lane == 0, ends, near0))
    add(press, 448, jnp.where(lane == EL - 1, ends, near1))
    for i in range(8):
        for f, j in ((0, 0), (1, 7)):
            at = i * 64 + j * 8
            add(press, at, near[i * 8 : i * 8 + 8, f * EL : (f + 1) * EL])
    wait_z(zs1, zr1, 1, 3, 0, False)
    for f, k in ((0, 0), (1, 7)):
        for h, at in enumerate(ends_of(press, 0, k)):
            press[at, :] = press[at, :] + zr1[1, f, :, h * 128 : h * 128 + 128]
    press_copies = [
        pltpu.make_async_copy(press.at[h * 512 : h * 512 + 512], press_hbm.at[:, h * 128 : h * 128 + 128], out_sem.at[2 + h])
        for h in range(2)
    ]
    for copy in press_copies:
        copy.start()
    for x in range(4):
        wait_links(x, True)
        if x < 2:
            for c in range(3):
                wait_z(zs, zr, x, x, c, True)
        else:
            wait_z(zs1, zr1, x - 2, x, 0, True)
    for copy in out_copies + press_copies:
        copy.wait()


def hand_over(first, second, first_out, second_out, sem):
    copies = []
    for q in range(PIECES):
        at = pl.ds(q * (1536 // PIECES), 1536 // PIECES)
        copies.append(pltpu.make_async_copy(first.at[at], first_out.at[at], sem.at[q]))
    copies.append(pltpu.make_async_copy(second, second_out, sem.at[PIECES]))
    for copy in copies:
        copy.start()
    for copy in copies:
        copy.wait()


def local(leaves, lobes, base_velocity, adjoint_velocity, element_size, link_slot):
    table, sums = constant_tables()
    rows = leaves * 8
    any_space = pl.BlockSpec(memory_space=pl.ANY)
    scratch = [
        pltpu.VMEM((1536, EL), F32),
        pltpu.VMEM((3072, 128), F32),
        pltpu.VMEM((3072, 128), F32),
        pltpu.VMEM((3072, 128), F32),
        pltpu.VMEM((9 * 512, EL), F32),
        pltpu.VMEM((1536, EL), F32),
        pltpu.VMEM((1024, 128), F32),
        pltpu.VMEM((10 * MODES, EL), F32),
        pltpu.VMEM((10 * MODES, EL), F32),
        pltpu.VMEM((1024, 128), F32),
        pltpu.VMEM((256, EL), F32),
        pltpu.VMEM((1, EL), F32),
        pltpu.VMEM((1, leaves * 4), jnp.int32),
        pltpu.VMEM((ROW_END, WIDE), BF16),
        pltpu.VMEM((MODES, 128), F32),
        pltpu.VMEM((2, 2, 192, EL), F32),
        pltpu.VMEM((2, 2, 192, EL), F32),
        pltpu.VMEM((2, 2, 64, EL), F32),
        pltpu.VMEM((2, 2, 64, EL), F32),
        pltpu.VMEM((4, rows, 128), F32),
        pltpu.VMEM((4, rows, 128), F32),
        pltpu.VMEM((rows, 512), BF16),
        pltpu.VMEM((rows, 512), BF16),
        pltpu.VMEM((rows, 384), BF16),
        pltpu.VMEM((rows, 768), BF16),
        pltpu.SemaphoreType.DMA((7,)),
        pltpu.SemaphoreType.DMA((4,)),
        pltpu.SemaphoreType.DMA((4, 2, 3)),
        pltpu.SemaphoreType.DMA((4, 2, 3)),
        pltpu.SemaphoreType.DMA((4,)),
        pltpu.SemaphoreType.DMA((4,)),
    ]
    out, press = pl.pallas_call(
        functools.partial(kernel, leaves, lobes),
        out_shape=(
            jax.ShapeDtypeStruct((1536, EL), F32),
            jax.ShapeDtypeStruct((512, EL), F32),
        ),
        in_specs=[any_space] * 6,
        out_specs=(any_space, any_space),
        scratch_shapes=scratch,
        compiler_params=pltpu.CompilerParams(
            collective_id=0, has_side_effects=True, vmem_limit_bytes=40 * 1024 * 1024
        ),
    )(
        *[
            pltpu.with_memory_space_constraint(one, pltpu.HBM)
            for one in (
                base_velocity.reshape(1536, EL),
                adjoint_velocity.reshape(1536, EL),
                element_size.reshape(1, EL),
                link_slot.reshape(1, leaves * 4),
                jnp.asarray(table),
                jnp.asarray(sums),
            )
        ]
    )
    out, press = pl.pallas_call(
        hand_over,
        out_shape=(
            pltpu.HBM((1536, EL), F32),
            pltpu.HBM((512, EL), F32),
        ),
        in_specs=[any_space] * 2,
        out_specs=(any_space, any_space),
        scratch_shapes=[pltpu.SemaphoreType.DMA((PIECES + 1,))],
        compiler_params=pltpu.CompilerParams(vmem_limit_bytes=32 * 1024 * 1024),
    )(out, press)
    return out.reshape(3, 512, EL), press


def solution(mesh):
    placed = (
        P(None, None, ("leaf", "lobe")),
        P(None, None, ("leaf", "lobe")),
        P(("leaf", "lobe")),
        P(("leaf", "lobe")),
    )
    return jax.shard_map(
        functools.partial(local, mesh.shape["leaf"], mesh.shape["lobe"]),
        mesh=mesh,
        in_specs=placed,
        out_specs=(P(None, None, ("leaf", "lobe")), P(None, ("leaf", "lobe"))),
        check_vma=False,
    )
```

```python
import functools
import math

import jax
import jax.numpy as jnp
import numpy as np
from jax import lax
from jax.experimental import pallas as pl
from jax.experimental.pallas import tpu as pltpu
from jax.sharding import PartitionSpec as P

NP = 8
PIECES = 1
EL = 256
MODES = 104
MODES16 = 112

time_step = 0.01
viscosity = 0.002
penalty = 0.5
shift_term = 1.0

F32 = jnp.float32
BF16 = jnp.bfloat16


def legendre_columns(points, degree):
    table = np.zeros((points.shape[0], degree + 1))
    table[:, 0] = 1.0
    table[:, 1] = points
    for order in range(2, degree + 1):
        table[:, order] = (
            (2 * order - 1) * points * table[:, order - 1] - (order - 1) * table[:, order - 2]
        ) / order
    return table


def node_tables():
    degree = NP - 1
    node_points = np.cos(np.pi * np.arange(degree + 1) / degree)
    for sweep in range(100):
        table = legendre_columns(node_points, degree)
        node_points = node_points - (node_points * table[:, degree] - table[:, degree - 1]) / (
            (degree + 1) * table[:, degree]
        )
    node_points = np.sort(node_points)
    values = legendre_columns(node_points, degree)[:, degree]
    matrix = np.zeros((NP, NP))
    for row_index in range(NP):
        for col_index in range(NP):
            if row_index != col_index:
                matrix[row_index, col_index] = values[row_index] / (
                    values[col_index] * (node_points[row_index] - node_points[col_index])
                )
    matrix[0, 0] = -degree * (degree + 1) / 4.0
    matrix[-1, -1] = degree * (degree + 1) / 4.0
    return matrix


def schwarz_tables():
    grid_count = NP + 2
    mode_index = np.arange(1, grid_count + 1)
    sine_basis = math.sqrt(2.0 / (grid_count + 1)) * np.sin(
        np.pi * np.outer(mode_index, mode_index) / (grid_count + 1)
    )
    eigen_values = 2.0 - 2.0 * np.cos(np.pi * mode_index / (grid_count + 1))
    return (sine_basis, eigen_values)


def three(matrix):
    high = matrix.astype(np.float32).astype(jnp.bfloat16)
    low = (matrix - high.astype(np.float64)).astype(np.float32).astype(jnp.bfloat16)
    return np.concatenate([high, low, high], axis=1)


WIDE = 384
ROW_JK, ROW_IK, ROW_DIV, ROW_INT, ROW_LAY, ROW_BACK = 0, 192, 320, 384, 496, 608
ROW_ALONG, ROW_FIX, ROW_END = 704, 784, 848


def constant_tables():
    diff = node_tables().astype(np.float32).astype(np.float64)
    sine, eigen = schwarz_tables()
    sine = sine.astype(np.float32).astype(np.float64)
    one = np.eye(NP)
    first, second = np.kron(diff, one), np.kron(one, diff)
    plane = np.concatenate([first, second, first @ first + second @ second], axis=0)
    along = np.concatenate([first, first @ first], axis=0)
    table = np.zeros((ROW_END, WIDE), jnp.bfloat16)
    table[ROW_JK : ROW_JK + 192, :192] = three(plane)
    table[ROW_IK : ROW_IK + 128, :192] = three(along)
    table[ROW_DIV : ROW_DIV + 64, :384] = np.concatenate([three(first), three(second)], axis=1)
    points = np.arange(64).reshape(8, 8)
    shell = np.concatenate([points[0], points[7], points[:, 0], points[:, 7]])
    put = np.zeros((64, 32))
    put[shell, np.arange(32)] = 1.0
    fix = np.concatenate([first @ put, second @ put], axis=1)
    table[ROW_FIX : ROW_FIX + 64, :192] = three(fix)
    table[ROW_FIX : ROW_FIX + 64, 192:256] = np.concatenate([put, put], axis=1)
    both = np.kron(sine, sine)
    grid = np.arange(100).reshape(10, 10)
    inner = grid[1:9, 1:9].reshape(-1)
    layers = np.concatenate([grid[0, 1:9], grid[9, 1:9], grid[1:9, 0], grid[1:9, 9]])
    forward = np.zeros((MODES16, 100))
    forward[:100] = both
    table[ROW_INT : ROW_INT + MODES16, :192] = three(forward[:, inner])
    table[ROW_LAY : ROW_LAY + MODES16, :96] = three(forward[:, layers])
    backward = np.zeros((96, MODES16))
    backward[:, :100] = both[np.concatenate([inner, layers])]
    table[ROW_BACK : ROW_BACK + 96, : 3 * MODES16] = three(backward)
    table[ROW_ALONG : ROW_ALONG + 80, :240] = three(np.kron(sine, one))
    sums = np.zeros((MODES,))
    sums[:100] = (eigen[:, None] + eigen[None, :]).reshape(-1)
    sums = np.tile(sums[:, None], (1, 128)).astype(np.float32)
    return table, sums


def split(x):
    high = x.astype(BF16)
    low = (x - high.astype(F32)).astype(BF16)
    return high, low


def both_parts(x):
    return jnp.concatenate(split(x), axis=1)


def stack(x):
    high, low = split(x)
    return jnp.concatenate([high, high, low], axis=0)


def ld(ref, at, size):
    half = ref.shape[0] // 2
    return jnp.concatenate([ref[pl.ds(at, size), :], ref[pl.ds(half + at, size), :]], axis=1)


def st(ref, at, value):
    half, size = ref.shape[0] // 2, value.shape[0]
    ref[pl.ds(at, size), :] = value[:, :128]
    ref[pl.ds(half + at, size), :] = value[:, 128:]


def add(ref, at, value):
    st(ref, at, ld(ref, at, value.shape[0]) + value)


def ends_of(ref, at, k):
    half = ref.shape[0] // 2
    return [pl.ds(h * half + at + k, 64, stride=8) for h in range(2)]


def dot(a, b):
    return lax.dot_general(a, b, (((1,), (0,)), ((), ())), preferred_element_type=F32)


def dot_nt(a, b):
    return lax.dot_general(a, b, (((1,), (1,)), ((), ())), preferred_element_type=F32)


def far_first(me, leaves):
    if leaves != 32:
        return [lax.rem(me + d, leaves) for d in range(1, leaves)]
    hops = [0, 1, 2, 1]
    steps = [(dy, dx, dc) for dy in range(4) for dx in range(4) for dc in range(2)][1:]
    steps.sort(key=lambda one: -(hops[one[0]] + hops[one[1]]))
    y, x, core = me // 8, lax.rem(me // 2, 4), lax.rem(me, 2)
    return [
        lax.rem(y + dy, 4) * 8 + lax.rem(x + dx, 4) * 2 + lax.rem(core + dc, 2)
        for dy, dx, dc in steps
    ]


def kernel(
    leaves, lobes,
    base_hbm, adj_hbm, size_hbm, slot_hbm, table_hbm, sums_hbm,
    out_hbm, press_hbm,
    base, v0, v1, v2, grads, part, res, modes, recip, press, outer,
    size, slot, table, sums,
    zs, zr, zs1, zr1, msg, recv, a_low, a_high, r_low, r_high, chain_in,
    in_sem, out_sem, z_send, z_recv, l_send, l_recv,
):
    me = lax.axis_index("leaf")
    lobe = lax.axis_index("lobe")
    rows = leaves * 8
    eigen = schwarz_tables()[1]

    barrier = pltpu.get_barrier_semaphore()
    peers = far_first(me, leaves)
    for peer in peers:
        pl.semaphore_signal(
            barrier, inc=1, device_id={"leaf": peer}, device_id_type=pl.DeviceIdType.MESH
        )

    @pl.when(lobe > 0)
    def _():
        pl.semaphore_signal(
            barrier, inc=1, device_id={"lobe": lobe - 1}, device_id_type=pl.DeviceIdType.MESH
        )

    @pl.when(lobe < lobes - 1)
    def _():
        pl.semaphore_signal(
            barrier, inc=1, device_id={"lobe": lobe + 1}, device_id_type=pl.DeviceIdType.MESH
        )

    loads = [pltpu.make_async_copy(slot_hbm, slot, in_sem.at[0])]
    for c in range(3):
        for h in range(2):
            loads.append(pltpu.make_async_copy(
                adj_hbm.at[c * 512 : c * 512 + 512, h * 128 : h * 128 + 128],
                v0.at[h * 1536 + c * 512 : h * 1536 + c * 512 + 512], in_sem.at[1 + c * 2 + h],
            ))
    loads += [
        pltpu.make_async_copy(table_hbm, table, in_sem.at[7]),
        pltpu.make_async_copy(size_hbm, size, in_sem.at[8]),
        pltpu.make_async_copy(base_hbm, base, in_sem.at[9]),
        pltpu.make_async_copy(sums_hbm, sums, in_sem.at[10]),
    ]
    for load in loads:
        load.start()

    for x in range(4):
        recv[x, pl.ds(pl.multiple_of(me * 8, 8), 8), :] = jnp.zeros((8, 128), F32)

    @pl.when(lobe == 0)
    def _():
        zr[:, 0] = jnp.zeros((2, 192, EL), F32)
        zr1[:, 0] = jnp.zeros((2, 64, EL), F32)

    @pl.when(lobe == lobes - 1)
    def _():
        zr[:, 1] = jnp.zeros((2, 192, EL), F32)
        zr1[:, 1] = jnp.zeros((2, 64, EL), F32)

    loads[0].wait()
    hot = (lax.broadcasted_iota(jnp.int32, (512, leaves * 4), 0) == slot[...]).astype(F32)
    row = lax.broadcasted_iota(jnp.int32, (rows, leaves * 4), 0)
    col = lax.broadcasted_iota(jnp.int32, (rows, leaves * 4), 1)
    spread = ((row >> 3) * 4 + (row & 3) == col).astype(F32)
    all_hot = dot_nt(spread.astype(BF16), hot.astype(BF16))
    low_row = (lax.broadcasted_iota(jnp.int32, (rows, 512), 0) & 4) == 0
    low_hot = jnp.where(low_row, all_hot, 0.0).astype(BF16)
    high_hot = jnp.where(low_row, 0.0, all_hot).astype(BF16)
    for part_at in range(2):
        a_low[:, part_at * 512 : part_at * 512 + 512] = low_hot
        a_high[:, part_at * 512 : part_at * 512 + 512] = high_hot
        r_low[part_at * rows : part_at * rows + rows, :] = low_hot
        r_high[part_at * rows : part_at * rows + rows, :] = high_hot
    for cc in range(3):
        row = lax.broadcasted_iota(jnp.int32, (rows, 128), 0)
        col = lax.broadcasted_iota(jnp.int32, (rows, 128), 1)
        after, before = (me + 1) * 8 + 4 + cc, (me - 1) * 8 + 4 + cc
        pick = ((row == after) & (col == 127)) | ((row == before) & (col == 0))
        pick = pick.astype(F32).astype(BF16)
        a_high[:, 1024 + cc * 256 : 1024 + cc * 256 + 128] = pick
        a_high[:, 1024 + cc * 256 + 128 : 1024 + cc * 256 + 256] = pick
        row = lax.broadcasted_iota(jnp.int32, (rows, EL), 0)
        col = lax.broadcasted_iota(jnp.int32, (rows, EL), 1)
        put = ((row == before) & (col == 0)) | ((row == after) & (col == EL - 1))
        put = put.astype(F32).astype(BF16)
        chain_in[0:rows, cc * EL : (cc + 1) * EL] = put
        chain_in[rows : 2 * rows, cc * EL : (cc + 1) * EL] = put

    def z_copies(sends, recvs, at, x, c):
        rows_of = pl.ds(c * 64, 64)
        up = pltpu.make_async_remote_copy(
            sends.at[at, 1, rows_of], recvs.at[at, 0, rows_of],
            z_send.at[x, 1, c], z_recv.at[x, 0, c],
            device_id={"lobe": lobe + 1}, device_id_type=pl.DeviceIdType.MESH,
        )
        down = pltpu.make_async_remote_copy(
            sends.at[at, 0, rows_of], recvs.at[at, 1, rows_of],
            z_send.at[x, 0, c], z_recv.at[x, 1, c],
            device_id={"lobe": lobe - 1}, device_id_type=pl.DeviceIdType.MESH,
        )
        return up, down

    def start_z(sends, recvs, at, x, c):
        up, down = z_copies(sends, recvs, at, x, c)

        @pl.when(lobe < lobes - 1)
        def _():
            up.start()

        @pl.when(lobe > 0)
        def _():
            down.start()

    def wait_z(sends, recvs, at, x, c, sent):
        up, down = z_copies(sends, recvs, at, x, c)

        @pl.when(lobe < lobes - 1)
        def _():
            up.wait_send() if sent else down.wait_recv()

        @pl.when(lobe > 0)
        def _():
            down.wait_send() if sent else up.wait_recv()

    def start_links(x):
        for peer in peers:
            pltpu.make_async_remote_copy(
                msg.at[x, pl.ds(pl.multiple_of(peer * 8, 8), 8)],
                recv.at[x, pl.ds(pl.multiple_of(me * 8, 8), 8)],
                l_send.at[x], l_recv.at[x],
                device_id={"leaf": peer}, device_id_type=pl.DeviceIdType.MESH,
            ).start()

    def wait_links(x, sent):
        copy = pltpu.make_async_remote_copy(
            msg.at[x, pl.ds(0, rows - 8)], recv.at[x, pl.ds(0, rows - 8)],
            l_send.at[x], l_recv.at[x],
            device_id={"leaf": lax.rem(me + 1, leaves)}, device_id_type=pl.DeviceIdType.MESH,
        )
        copy.wait_send() if sent else copy.wait_recv()

    def low_message(face2, face3):
        return dot_nt(a_low[...], both_parts(jnp.concatenate([face2, face3], axis=1)))

    def fill_message(x, total, face2, face3, leads, tails):
        end_lane = lax.broadcasted_iota(jnp.int32, (64, 128), 1)
        ends = [
            jnp.where(end_lane == 0, lead, jnp.where(end_lane == 127, tail, 0.0))
            for lead, tail in zip(leads, tails)
        ]
        faces = both_parts(jnp.concatenate([face2, face3], axis=1))
        ends = jnp.concatenate([both_parts(one) for one in ends], axis=1)
        width = ends.shape[1]
        right = jnp.concatenate(
            [
                jnp.concatenate([faces, jnp.zeros((64, width), BF16)], axis=1),
                jnp.concatenate([jnp.zeros((64, 1024), BF16), ends], axis=1),
            ],
            axis=0,
        )
        high = dot_nt(a_high[:, : 1024 + width], right)
        msg[x] = high if total is None else total + high

    def read_links(x, count):
        parts = both_parts(jnp.transpose(recv[x]))
        near = dot(parts[:64], r_high[...])
        if count == 3:
            near = jnp.concatenate([dot(parts, r_low[...]), near], axis=0)
        return near, dot(parts[64:], chain_in[:, : count * EL])

    def spot(c, i):
        return pl.multiple_of(c * 512 + i * 64, 64)

    def block(c, i):
        return pl.ds(spot(c, i), 64)

    def across(ref, c, j):
        at = [pl.multiple_of(c * 512 + i * 64 + j * 8, 8) for i in range(8)]
        if ref.shape[1] == 128:
            return jnp.concatenate([ld(ref, one, 8) for one in at], axis=0)
        return jnp.concatenate([ref[pl.ds(one, 8), :] for one in at], axis=0)

    def put_across(ref, c, j, value):
        for i in range(8):
            at = pl.multiple_of(c * 512 + i * 64 + j * 8, 8)
            if ref.shape[1] == 128:
                st(ref, at, value[i * 8 : i * 8 + 8])
            else:
                ref[pl.ds(at, 8), :] = value[i * 8 : i * 8 + 8]

    lane = lax.broadcasted_iota(jnp.int32, (64, EL), 1)

    def chain_near(lead, tail):
        near0 = jnp.where(lane == 0, 0.0, pltpu.roll(tail, 1, 1))
        near1 = jnp.where(lane == EL - 1, 0.0, pltpu.roll(lead, EL - 1, 1))
        return near0, near1

    def side(v, parts, j):
        return jnp.concatenate(
            [ld(v, c * 512 + i * 64 + j * 8, 8) for c in parts for i in range(8)], axis=0
        )

    def low_faces(v):
        return low_message(side(v, (0, 1), 0), side(v, (0, 1), 7))

    def send_links(v, x, total):
        leads = [v[c * 512 : c * 512 + 64, :] for c in range(3)]
        tails = [v[1536 + c * 512 + 448 : 1536 + c * 512 + 512, :] for c in range(3)]
        fill_message(x, total, side(v, (2,), 0), side(v, (2,), 7), leads, tails)
        if x == 0:
            pl.semaphore_wait(
                barrier,
                leaves - 1 + (lobe > 0).astype(jnp.int32) + (lobe < lobes - 1).astype(jnp.int32),
            )
            for c in range(3):
                start_z(zs, zr, 0, 0, c)
        start_links(x)

    def advance(v, w):
        scale = 2.0 / size[...]
        visc = viscosity * scale
        step = time_step * scale

        def one(j, carry):
            for c in range(3):
                y = dot(table[ROW_IK : ROW_IK + 128, :192], stack(across(v, c, j)))
                put_across(part, c, j, across(base, 0, j) * y[:64] + visc * y[64:])
            return carry

        lax.fori_loop(0, 8, one, 0, unroll=2)
        sub = lax.broadcasted_iota(jnp.int32, (64, EL), 0)
        k, j = sub & 7, sub >> 3
        edge = ((k == 0) | (k == 7)).astype(F32) + ((j == 0) | (j == 7)).astype(F32)

        def two(i, carry):
            own = [ld(v, spot(r, i), 64) for r in range(3)]
            b1, b2 = base[block(1, i), :], base[block(2, i), :]
            ends = jnp.where((i == 0) | (i == 7), 1.0, 0.0).astype(F32)
            keep = 1.0 - penalty * (edge + ends)
            for c in range(3):
                y = dot(table[ROW_JK : ROW_JK + 192, :192], stack(own[c]))
                total = part[block(c, i), :] + b1 * y[:64] + b2 * y[64:128] + visc * y[128:]
                for r in range(3):
                    total -= own[r] * grads[block(c * 3 + r, i), :]
                st(w, spot(c, i), keep * own[c] + step * total)
            return carry

        lax.fori_loop(0, 8, two, 0, unroll=2)
        for c in range(3):
            near0, near1 = chain_near(ld(v, spot(c, 0), 64), ld(v, spot(c, 7), 64))
            add(w, spot(c, 0), penalty * near0)
            add(w, spot(c, 7), penalty * near1)
    def add_links(w, near, ends):
        for c in range(3):
            end = ends[:, c * EL : (c + 1) * EL]
            add(w, spot(c, 0), jnp.where(lane == 0, penalty * end, 0.0))
            add(w, spot(c, 7), jnp.where(lane == EL - 1, penalty * end, 0.0))
            for i in range(8):
                for f, j in ((0, 0), (1, 7)):
                    r0 = c * 64 + i * 8
                    add(
                        w, c * 512 + i * 64 + j * 8,
                        penalty * near[r0 : r0 + 8, f * EL : (f + 1) * EL],
                    )

    def add_z(w, x, c):
        for f, k in ((0, 0), (1, 7)):
            for h, at in enumerate(ends_of(w, c * 512, k)):
                here = slice(c * 64, c * 64 + 64), slice(h * 128, h * 128 + 128)
                value = w[at, :] + penalty * zr[x, f, here[0], here[1]]
                w[at, :] = value
                if x == 0:
                    zs[1, f, here[0], here[1]] = value

    for c in range(3):
        loads[1 + 2 * c].wait()
        loads[2 + 2 * c].wait()
        for f, k in ((0, 0), (1, 7)):
            for h, at in enumerate(ends_of(v0, c * 512, k)):
                zs[0, f, c * 64 : c * 64 + 64, h * 128 : h * 128 + 128] = v0[at, :]
    send_links(v0, 0, low_faces(v0))
    for load in loads[7:]:
        load.wait()

    def grad_one(j, carry):
        for r in range(3):
            y = dot(table[ROW_IK : ROW_IK + 64, :192], stack(across(base, r, j)))
            put_across(grads, r, j, y)
        return carry

    lax.fori_loop(0, 8, grad_one, 0, unroll=2)

    def grad_two(i, carry):
        for r in range(3):
            y = dot(table[ROW_JK : ROW_JK + 128, :192], stack(base[block(r, i), :]))
            grads[block(3 + r, i), :] = y[:64]
            grads[block(6 + r, i), :] = y[64:]
        return carry

    lax.fori_loop(0, 8, grad_two, 0, unroll=2)
    advance(v0, v1)
    wait_links(0, False)
    add_links(v1, *read_links(0, 3))
    total = None
    for c in range(3):
        wait_z(zs, zr, 0, 0, c, False)
        add_z(v1, 0, c)
        start_z(zs, zr, 1, 1, c)
        if c == 1:
            total = low_faces(v1)
    send_links(v1, 1, total)

    scale_square = (1.0 / size[...]) ** 2

    def recip_body(b, carry):
        at = pl.multiple_of(b * 8, 8)
        here = sums[pl.ds(at, 8), :]
        here = jnp.concatenate([here, here], axis=1)
        for m in range(10):
            recip[pl.ds(pl.multiple_of(m * MODES + at, 8), 8), :] = 1.0 / (
                (here + float(eigen[m])) * scale_square + shift_term
            )
        return carry

    lax.fori_loop(0, MODES // 8, recip_body, 0)
    advance(v1, v2)

    scale = 2.0 / size[...]

    def div_one(j, carry):
        put_across(res, 0, j, dot(table[ROW_IK : ROW_IK + 64, :192], stack(across(v2, 0, j))))
        return carry

    lax.fori_loop(0, 8, div_one, 0, unroll=4)

    def div_pair(first_part, second_part):
        both = jnp.concatenate([stack(first_part), stack(second_part)], axis=0)
        return dot(table[ROW_DIV : ROW_DIV + 64, :], both)

    def div_two(i, carry):
        add(res, spot(0, i), div_pair(ld(v2, spot(1, i), 64), ld(v2, spot(2, i), 64)))
        return carry

    lax.fori_loop(0, 8, div_two, 0, unroll=4)

    wait_links(1, False)
    near, ends = read_links(1, 3)
    end0 = [jnp.where(lane == 0, penalty * ends[:, c * EL : (c + 1) * EL], 0.0) for c in range(3)]
    end1 = [
        jnp.where(lane == EL - 1, penalty * ends[:, c * EL : (c + 1) * EL], 0.0) for c in range(3)
    ]
    ends_fix = {0: div_pair(end0[1], end0[2]), 7: div_pair(end1[1], end1[2])}
    for c in range(3):
        wait_z(zs, zr, 1, 1, c, False)

    def shell(c, f):
        here = slice(c * 64, c * 64 + 64)
        if f < 2:
            return penalty * near[here, f * EL : (f + 1) * EL]
        return penalty * zr[1, f - 2, here, :]

    shells = [[shell(c, f) for f in range(4)] for c in range(3)]
    along_i = [dot(table[ROW_IK : ROW_IK + 64, :192], stack(one)) for one in shells[0]]
    diff = node_tables()
    for i in range(8):
        r0 = slice(i * 8, i * 8 + 8)
        plane = jnp.concatenate([shells[c][f][r0] for c in (1, 2) for f in range(4)], axis=0)
        rest = split(jnp.concatenate([one[r0] for one in along_i], axis=0))
        y = dot(
            table[ROW_FIX : ROW_FIX + 64, :256], jnp.concatenate([stack(plane), *rest], axis=0)
        )
        y += float(diff[i, 0]) * end0[0] + float(diff[i, 7]) * end1[0]
        if i in ends_fix:
            y += ends_fix[i]
        st(res, i * 64, scale * (ld(res, i * 64, 64) + y))
    face2 = jnp.concatenate([ld(res, i * 64, 8) for i in range(8)], axis=0)
    face3 = jnp.concatenate([ld(res, i * 64 + 56, 8) for i in range(8)], axis=0)
    fill_message(2, None, face2, face3, [res[0:64, :]], [res[512 + 448 : 512 + 512, :]])
    start_links(2)
    for f, k in ((0, 0), (1, 7)):
        for h, at in enumerate(ends_of(res, 0, k)):
            zs1[0, f, :, h * 128 : h * 128 + 128] = res[at, :]
    start_z(zs1, zr1, 0, 2, 0)

    add_links(v2, near, ends)
    for c in range(3):
        add_z(v2, 1, c)
    out_copies = [
        pltpu.make_async_copy(
            v2.at[h * 1536 : h * 1536 + 1536], out_hbm.at[:, h * 128 : h * 128 + 128], out_sem.at[h]
        )
        for h in range(2)
    ]
    for copy in out_copies:
        copy.start()

    def forward(i, carry):
        y = dot(table[ROW_INT : ROW_INT + MODES16, :192], stack(ld(res, spot(0, i), 64)))
        modes[pl.ds(pl.multiple_of((i + 1) * MODES, 8), MODES), :] = y[:MODES]
        return carry

    lax.fori_loop(0, 8, forward, 0, unroll=4)
    near0, near1 = chain_near(ld(res, 0, 64), ld(res, 448, 64))
    wait_links(2, False)
    near, ends = read_links(2, 1)
    near0 = jnp.where(lane == 0, ends, near0)
    near1 = jnp.where(lane == EL - 1, ends, near1)
    for n, plane in ((0, near0), (9, near1)):
        y = dot(table[ROW_INT : ROW_INT + MODES16, :192], stack(plane))
        modes[n * MODES : (n + 1) * MODES, :] = y[:MODES]
    wait_z(zs1, zr1, 0, 2, 0, False)
    for i in range(8):
        r0 = slice(i * 8, i * 8 + 8)
        layer = jnp.concatenate(
            [near[r0, :EL], near[r0, EL:], zr1[0, 0, r0, :], zr1[0, 1, r0, :]], axis=0
        )
        y = dot(table[ROW_LAY : ROW_LAY + MODES16, :96], stack(layer))
        modes[(i + 1) * MODES : (i + 2) * MODES, :] += y[:MODES]

    along = table[ROW_ALONG : ROW_ALONG + 80, :240]

    def solve(b, carry):
        at = [pl.ds(pl.multiple_of(m * MODES + b * 8, 8), 8) for m in range(10)]
        values = jnp.concatenate([modes[one, :] for one in at], axis=0)
        values = dot(along, stack(values))
        values = values * jnp.concatenate([recip[one, :] for one in at], axis=0)
        values = dot(along, stack(values))
        for m in range(10):
            modes[at[m], :] = values[m * 8 : m * 8 + 8]
        return carry

    lax.fori_loop(0, MODES // 8, solve, 0, unroll=MODES // 8)

    pad = jnp.zeros((MODES16 - MODES, EL), F32)

    def mode_plane(n):
        plane = modes[pl.ds(pl.multiple_of(n * MODES, 8), MODES), :]
        return stack(jnp.concatenate([plane, pad], axis=0))

    for i in range(8):
        y = dot(table[ROW_BACK + 64 : ROW_BACK + 96, : 3 * MODES16], mode_plane(i + 1))
        r0 = slice(i * 8, i * 8 + 8)
        outer[128 + i * 8 : 136 + i * 8, :] = y[0:8]
        outer[192 + i * 8 : 200 + i * 8, :] = y[8:16]
        zs1[1, 0, r0, :] = y[16:24]
        zs1[1, 1, r0, :] = y[24:32]
    for n, at in ((0, 0), (9, 64)):
        outer[at : at + 64, :] = dot(table[ROW_BACK : ROW_BACK + 64, : 3 * MODES16], mode_plane(n))
    fill_message(
        3, None, outer[128:192, :], outer[192:256, :],
        [outer[0:64, 0:128]], [outer[64:128, 128:256]],
    )
    start_links(3)
    start_z(zs1, zr1, 1, 3, 0)

    def backward(i, carry):
        st(press, spot(0, i), dot(table[ROW_BACK : ROW_BACK + 64, : 3 * MODES16], mode_plane(i + 1)))
        return carry

    lax.fori_loop(0, 8, backward, 0, unroll=4)
    near0, near1 = chain_near(outer[0:64, :], outer[64:128, :])
    wait_links(3, False)
    near, ends = read_links(3, 1)
    add(press, 0, jnp.where(lane == 0, ends, near0))
    add(press, 448, jnp.where(lane == EL - 1, ends, near1))
    for i in range(8):
        for f, j in ((0, 0), (1, 7)):
            at = i * 64 + j * 8
            add(press, at, near[i * 8 : i * 8 + 8, f * EL : (f + 1) * EL])
    wait_z(zs1, zr1, 1, 3, 0, False)
    press_copies = []
    for h in range(2):
        for f, k in ((0, 0), (1, 7)):
            at = ends_of(press, 0, k)[h]
            press[at, :] = press[at, :] + zr1[1, f, :, h * 128 : h * 128 + 128]
        copy = pltpu.make_async_copy(
            press.at[h * 512 : h * 512 + 512], press_hbm.at[:, h * 128 : h * 128 + 128], out_sem.at[2 + h]
        )
        copy.start()
        press_copies.append(copy)
    for x in range(4):
        wait_links(x, True)
        if x < 2:
            for c in range(3):
                wait_z(zs, zr, x, x, c, True)
        else:
            wait_z(zs1, zr1, x - 2, x, 0, True)
    for copy in out_copies + press_copies:
        copy.wait()


def hand_over(first, second, first_out, second_out, sem):
    copies = []
    for q in range(PIECES):
        at = pl.ds(q * (1536 // PIECES), 1536 // PIECES)
        copies.append(pltpu.make_async_copy(first.at[at], first_out.at[at], sem.at[q]))
    copies.append(pltpu.make_async_copy(second, second_out, sem.at[PIECES]))
    for copy in copies:
        copy.start()
    for copy in copies:
        copy.wait()


def local(leaves, lobes, base_velocity, adjoint_velocity, element_size, link_slot):
    table, sums = constant_tables()
    rows = leaves * 8
    any_space = pl.BlockSpec(memory_space=pl.ANY)
    scratch = [
        pltpu.VMEM((1536, EL), F32),
        pltpu.VMEM((3072, 128), F32),
        pltpu.VMEM((3072, 128), F32),
        pltpu.VMEM((3072, 128), F32),
        pltpu.VMEM((9 * 512, EL), F32),
        pltpu.VMEM((1536, EL), F32),
        pltpu.VMEM((1024, 128), F32),
        pltpu.VMEM((10 * MODES, EL), F32),
        pltpu.VMEM((10 * MODES, EL), F32),
        pltpu.VMEM((1024, 128), F32),
        pltpu.VMEM((256, EL), F32),
        pltpu.VMEM((1, EL), F32),
        pltpu.VMEM((1, leaves * 4), jnp.int32),
        pltpu.VMEM((ROW_END, WIDE), BF16),
        pltpu.VMEM((MODES, 128), F32),
        pltpu.VMEM((2, 2, 192, EL), F32),
        pltpu.VMEM((2, 2, 192, EL), F32),
        pltpu.VMEM((2, 2, 64, EL), F32),
        pltpu.VMEM((2, 2, 64, EL), F32),
        pltpu.VMEM((4, rows, 128), F32),
        pltpu.VMEM((4, rows, 128), F32),
        pltpu.VMEM((rows, 1024), BF16),
        pltpu.VMEM((rows, 1792), BF16),
        pltpu.VMEM((2 * rows, 512), BF16),
        pltpu.VMEM((2 * rows, 512), BF16),
        pltpu.VMEM((2 * rows, 768), BF16),
        pltpu.SemaphoreType.DMA((11,)),
        pltpu.SemaphoreType.DMA((4,)),
        pltpu.SemaphoreType.DMA((4, 2, 3)),
        pltpu.SemaphoreType.DMA((4, 2, 3)),
        pltpu.SemaphoreType.DMA((4,)),
        pltpu.SemaphoreType.DMA((4,)),
    ]
    out, press = pl.pallas_call(
        functools.partial(kernel, leaves, lobes),
        out_shape=(
            jax.ShapeDtypeStruct((1536, EL), F32),
            jax.ShapeDtypeStruct((512, EL), F32),
        ),
        in_specs=[any_space] * 6,
        out_specs=(any_space, any_space),
        scratch_shapes=scratch,
        compiler_params=pltpu.CompilerParams(
            collective_id=0, has_side_effects=True, vmem_limit_bytes=40 * 1024 * 1024
        ),
    )(
        *[
            pltpu.with_memory_space_constraint(one, pltpu.HBM)
            for one in (
                base_velocity.reshape(1536, EL),
                adjoint_velocity.reshape(1536, EL),
                element_size.reshape(1, EL),
                link_slot.reshape(1, leaves * 4),
                jnp.asarray(table),
                jnp.asarray(sums),
            )
        ]
    )
    out, press = pl.pallas_call(
        hand_over,
        out_shape=(
            pltpu.HBM((1536, EL), F32),
            pltpu.HBM((512, EL), F32),
        ),
        in_specs=[any_space] * 2,
        out_specs=(any_space, any_space),
        scratch_shapes=[pltpu.SemaphoreType.DMA((PIECES + 1,))],
        compiler_params=pltpu.CompilerParams(vmem_limit_bytes=32 * 1024 * 1024),
    )(out, press)
    return out.reshape(3, 512, EL), press


def solution(mesh):
    placed = (
        P(None, None, ("leaf", "lobe")),
        P(None, None, ("leaf", "lobe")),
        P(("leaf", "lobe")),
        P(("leaf", "lobe")),
    )
    return jax.shard_map(
        functools.partial(local, mesh.shape["leaf"], mesh.shape["lobe"]),
        mesh=mesh,
        in_specs=placed,
        out_specs=(P(None, None, ("leaf", "lobe")), P(None, ("leaf", "lobe"))),
        check_vma=False,
    )
```

```python
import functools
import math

import jax
import jax.numpy as jnp
import numpy as np
from jax import lax
from jax.experimental import pallas as pl
from jax.experimental.pallas import tpu as pltpu
from jax.sharding import PartitionSpec as P

NP = 8
PIECES = 1
EL = 256
MODES = 104
MODES16 = 112

time_step = 0.01
viscosity = 0.002
penalty = 0.5
shift_term = 1.0

F32 = jnp.float32
BF16 = jnp.bfloat16


def legendre_columns(points, degree):
    table = np.zeros((points.shape[0], degree + 1))
    table[:, 0] = 1.0
    table[:, 1] = points
    for order in range(2, degree + 1):
        table[:, order] = (
            (2 * order - 1) * points * table[:, order - 1] - (order - 1) * table[:, order - 2]
        ) / order
    return table


def node_tables():
    degree = NP - 1
    node_points = np.cos(np.pi * np.arange(degree + 1) / degree)
    for sweep in range(100):
        table = legendre_columns(node_points, degree)
        node_points = node_points - (node_points * table[:, degree] - table[:, degree - 1]) / (
            (degree + 1) * table[:, degree]
        )
    node_points = np.sort(node_points)
    values = legendre_columns(node_points, degree)[:, degree]
    matrix = np.zeros((NP, NP))
    for row_index in range(NP):
        for col_index in range(NP):
            if row_index != col_index:
                matrix[row_index, col_index] = values[row_index] / (
                    values[col_index] * (node_points[row_index] - node_points[col_index])
                )
    matrix[0, 0] = -degree * (degree + 1) / 4.0
    matrix[-1, -1] = degree * (degree + 1) / 4.0
    return matrix


def schwarz_tables():
    grid_count = NP + 2
    mode_index = np.arange(1, grid_count + 1)
    sine_basis = math.sqrt(2.0 / (grid_count + 1)) * np.sin(
        np.pi * np.outer(mode_index, mode_index) / (grid_count + 1)
    )
    eigen_values = 2.0 - 2.0 * np.cos(np.pi * mode_index / (grid_count + 1))
    return (sine_basis, eigen_values)


def three(matrix):
    high = matrix.astype(np.float32).astype(jnp.bfloat16)
    low = (matrix - high.astype(np.float64)).astype(np.float32).astype(jnp.bfloat16)
    return np.concatenate([high, low, high], axis=1)


WIDE = 384
ROW_JK, ROW_IK, ROW_DIV, ROW_INT, ROW_LAY, ROW_BACK = 0, 192, 320, 384, 496, 608
ROW_ALONG, ROW_FIX, ROW_END = 704, 784, 848


def constant_tables():
    diff = node_tables().astype(np.float32).astype(np.float64)
    sine, eigen = schwarz_tables()
    sine = sine.astype(np.float32).astype(np.float64)
    one = np.eye(NP)
    first, second = np.kron(diff, one), np.kron(one, diff)
    plane = np.concatenate([first, second, first @ first + second @ second], axis=0)
    along = np.concatenate([first, first @ first], axis=0)
    table = np.zeros((ROW_END, WIDE), jnp.bfloat16)
    table[ROW_JK : ROW_JK + 192, :192] = three(plane)
    table[ROW_IK : ROW_IK + 128, :192] = three(along)
    table[ROW_DIV : ROW_DIV + 64, :384] = np.concatenate([three(first), three(second)], axis=1)
    points = np.arange(64).reshape(8, 8)
    shell = np.concatenate([points[0], points[7], points[:, 0], points[:, 7]])
    put = np.zeros((64, 32))
    put[shell, np.arange(32)] = 1.0
    fix = np.concatenate([first @ put, second @ put], axis=1)
    table[ROW_FIX : ROW_FIX + 64, :192] = three(fix)
    table[ROW_FIX : ROW_FIX + 64, 192:256] = np.concatenate([put, put], axis=1)
    both = np.kron(sine, sine)
    grid = np.arange(100).reshape(10, 10)
    inner = grid[1:9, 1:9].reshape(-1)
    layers = np.concatenate([grid[0, 1:9], grid[9, 1:9], grid[1:9, 0], grid[1:9, 9]])
    forward = np.zeros((MODES16, 100))
    forward[:100] = both
    table[ROW_INT : ROW_INT + MODES16, :192] = three(forward[:, inner])
    table[ROW_LAY : ROW_LAY + MODES16, :96] = three(forward[:, layers])
    backward = np.zeros((96, MODES16))
    backward[:, :100] = both[np.concatenate([inner, layers])]
    table[ROW_BACK : ROW_BACK + 96, : 3 * MODES16] = three(backward)
    table[ROW_ALONG : ROW_ALONG + 80, :240] = three(np.kron(sine, one))
    sums = np.zeros((MODES,))
    sums[:100] = (eigen[:, None] + eigen[None, :]).reshape(-1)
    sums = np.tile(sums[:, None], (1, 128)).astype(np.float32)
    return table, sums


def split(x):
    high = x.astype(BF16)
    low = (x - high.astype(F32)).astype(BF16)
    return high, low


def both_parts(x):
    return jnp.concatenate(split(x), axis=1)


def stack(x):
    high, low = split(x)
    return jnp.concatenate([high, high, low], axis=0)


def ld(ref, at, size):
    half = ref.shape[0] // 2
    return jnp.concatenate([ref[pl.ds(at, size), :], ref[pl.ds(half + at, size), :]], axis=1)


def st(ref, at, value):
    half, size = ref.shape[0] // 2, value.shape[0]
    ref[pl.ds(at, size), :] = value[:, :128]
    ref[pl.ds(half + at, size), :] = value[:, 128:]


def add(ref, at, value):
    st(ref, at, ld(ref, at, value.shape[0]) + value)


def ends_of(ref, at, k):
    half = ref.shape[0] // 2
    return [pl.ds(h * half + at + k, 64, stride=8) for h in range(2)]


def dot(a, b):
    return lax.dot_general(a, b, (((1,), (0,)), ((), ())), preferred_element_type=F32)


def dot_nt(a, b):
    return lax.dot_general(a, b, (((1,), (1,)), ((), ())), preferred_element_type=F32)


def far_first(me, leaves):
    if leaves != 32:
        return [lax.rem(me + d, leaves) for d in range(1, leaves)]
    hops = [0, 1, 2, 1]
    steps = [(dy, dx, dc) for dy in range(4) for dx in range(4) for dc in range(2)][1:]
    steps.sort(key=lambda one: -(hops[one[0]] + hops[one[1]]))
    y, x, core = me // 8, lax.rem(me // 2, 4), lax.rem(me, 2)
    return [
        lax.rem(y + dy, 4) * 8 + lax.rem(x + dx, 4) * 2 + lax.rem(core + dc, 2)
        for dy, dx, dc in steps
    ]


def kernel(
    leaves, lobes,
    base_hbm, adj_hbm, size_hbm, slot_hbm, table_hbm, sums_hbm,
    out_hbm, press_hbm,
    base, v0, v1, v2, grads, part, res, modes, recip, press, outer,
    size, slot, table, sums,
    zs, zr, zs1, zr1, msg, recv, a_low, a_high, r_low, r_high, chain_in,
    in_sem, out_sem, z_send, z_recv, l_send, l_recv,
):
    me = lax.axis_index("leaf")
    lobe = lax.axis_index("lobe")
    rows = leaves * 8
    eigen = schwarz_tables()[1]

    barrier = pltpu.get_barrier_semaphore()
    peers = far_first(me, leaves)
    for peer in peers:
        pl.semaphore_signal(
            barrier, inc=1, device_id={"leaf": peer}, device_id_type=pl.DeviceIdType.MESH
        )

    @pl.when(lobe > 0)
    def _():
        pl.semaphore_signal(
            barrier, inc=1, device_id={"lobe": lobe - 1}, device_id_type=pl.DeviceIdType.MESH
        )

    @pl.when(lobe < lobes - 1)
    def _():
        pl.semaphore_signal(
            barrier, inc=1, device_id={"lobe": lobe + 1}, device_id_type=pl.DeviceIdType.MESH
        )

    loads = [pltpu.make_async_copy(slot_hbm, slot, in_sem.at[0])]
    for c in range(3):
        for h in range(2):
            loads.append(pltpu.make_async_copy(
                adj_hbm.at[c * 512 : c * 512 + 512, h * 128 : h * 128 + 128],
                v0.at[h * 1536 + c * 512 : h * 1536 + c * 512 + 512], in_sem.at[1 + c * 2 + h],
            ))
    loads += [
        pltpu.make_async_copy(table_hbm, table, in_sem.at[7]),
        pltpu.make_async_copy(size_hbm, size, in_sem.at[8]),
        pltpu.make_async_copy(base_hbm, base, in_sem.at[9]),
        pltpu.make_async_copy(sums_hbm, sums, in_sem.at[10]),
    ]
    for load in loads[:7]:
        load.start()

    for x in range(4):
        recv[x, pl.ds(pl.multiple_of(me * 8, 8), 8), :] = jnp.zeros((8, 128), F32)

    @pl.when(lobe == 0)
    def _():
        zr[:, 0] = jnp.zeros((2, 192, EL), F32)
        zr1[:, 0] = jnp.zeros((2, 64, EL), F32)

    @pl.when(lobe == lobes - 1)
    def _():
        zr[:, 1] = jnp.zeros((2, 192, EL), F32)
        zr1[:, 1] = jnp.zeros((2, 64, EL), F32)

    loads[0].wait()
    hot = (lax.broadcasted_iota(jnp.int32, (512, leaves * 4), 0) == slot[...]).astype(F32)
    row = lax.broadcasted_iota(jnp.int32, (rows, leaves * 4), 0)
    col = lax.broadcasted_iota(jnp.int32, (rows, leaves * 4), 1)
    spread = ((row >> 3) * 4 + (row & 3) == col).astype(F32)
    all_hot = dot_nt(spread.astype(BF16), hot.astype(BF16))
    low_row = (lax.broadcasted_iota(jnp.int32, (rows, 512), 0) & 4) == 0
    low_hot = jnp.where(low_row, all_hot, 0.0).astype(BF16)
    high_hot = jnp.where(low_row, 0.0, all_hot).astype(BF16)
    for part_at in range(2):
        a_low[:, part_at * 512 : part_at * 512 + 512] = low_hot
        a_high[:, part_at * 512 : part_at * 512 + 512] = high_hot
        r_low[part_at * rows : part_at * rows + rows, :] = low_hot
        r_high[part_at * rows : part_at * rows + rows, :] = high_hot
    for cc in range(3):
        row = lax.broadcasted_iota(jnp.int32, (rows, 128), 0)
        col = lax.broadcasted_iota(jnp.int32, (rows, 128), 1)
        after, before = (me + 1) * 8 + 4 + cc, (me - 1) * 8 + 4 + cc
        pick = ((row == after) & (col == 127)) | ((row == before) & (col == 0))
        pick = pick.astype(F32).astype(BF16)
        a_high[:, 1024 + cc * 256 : 1024 + cc * 256 + 128] = pick
        a_high[:, 1024 + cc * 256 + 128 : 1024 + cc * 256 + 256] = pick
        row = lax.broadcasted_iota(jnp.int32, (rows, EL), 0)
        col = lax.broadcasted_iota(jnp.int32, (rows, EL), 1)
        put = ((row == before) & (col == 0)) | ((row == after) & (col == EL - 1))
        put = put.astype(F32).astype(BF16)
        chain_in[0:rows, cc * EL : (cc + 1) * EL] = put
        chain_in[rows : 2 * rows, cc * EL : (cc + 1) * EL] = put

    def z_copies(sends, recvs, at, x, c):
        rows_of = pl.ds(c * 64, 64)
        up = pltpu.make_async_remote_copy(
            sends.at[at, 1, rows_of], recvs.at[at, 0, rows_of],
            z_send.at[x, 1, c], z_recv.at[x, 0, c],
            device_id={"lobe": lobe + 1}, device_id_type=pl.DeviceIdType.MESH,
        )
        down = pltpu.make_async_remote_copy(
            sends.at[at, 0, rows_of], recvs.at[at, 1, rows_of],
            z_send.at[x, 0, c], z_recv.at[x, 1, c],
            device_id={"lobe": lobe - 1}, device_id_type=pl.DeviceIdType.MESH,
        )
        return up, down

    def start_z(sends, recvs, at, x, c):
        up, down = z_copies(sends, recvs, at, x, c)

        @pl.when(lobe < lobes - 1)
        def _():
            up.start()

        @pl.when(lobe > 0)
        def _():
            down.start()

    def wait_z(sends, recvs, at, x, c, sent):
        up, down = z_copies(sends, recvs, at, x, c)

        @pl.when(lobe < lobes - 1)
        def _():
            up.wait_send() if sent else down.wait_recv()

        @pl.when(lobe > 0)
        def _():
            down.wait_send() if sent else up.wait_recv()

    def start_links(x):
        for peer in peers:
            pltpu.make_async_remote_copy(
                msg.at[x, pl.ds(pl.multiple_of(peer * 8, 8), 8)],
                recv.at[x, pl.ds(pl.multiple_of(me * 8, 8), 8)],
                l_send.at[x], l_recv.at[x],
                device_id={"leaf": peer}, device_id_type=pl.DeviceIdType.MESH,
            ).start()

    def wait_links(x, sent):
        copy = pltpu.make_async_remote_copy(
            msg.at[x, pl.ds(0, rows - 8)], recv.at[x, pl.ds(0, rows - 8)],
            l_send.at[x], l_recv.at[x],
            device_id={"leaf": lax.rem(me + 1, leaves)}, device_id_type=pl.DeviceIdType.MESH,
        )
        copy.wait_send() if sent else copy.wait_recv()

    def low_message(face2, face3):
        return dot_nt(a_low[...], both_parts(jnp.concatenate([face2, face3], axis=1)))

    def fill_message(x, total, face2, face3, leads, tails):
        end_lane = lax.broadcasted_iota(jnp.int32, (64, 128), 1)
        ends = [
            jnp.where(end_lane == 0, lead, jnp.where(end_lane == 127, tail, 0.0))
            for lead, tail in zip(leads, tails)
        ]
        faces = both_parts(jnp.concatenate([face2, face3], axis=1))
        ends = jnp.concatenate([both_parts(one) for one in ends], axis=1)
        width = ends.shape[1]
        right = jnp.concatenate(
            [
                jnp.concatenate([faces, jnp.zeros((64, width), BF16)], axis=1),
                jnp.concatenate([jnp.zeros((64, 1024), BF16), ends], axis=1),
            ],
            axis=0,
        )
        high = dot_nt(a_high[:, : 1024 + width], right)
        msg[x] = high if total is None else total + high

    def read_links(x, count):
        parts = both_parts(jnp.transpose(recv[x]))
        near = dot(parts[:64], r_high[...])
        if count == 3:
            near = jnp.concatenate([dot(parts, r_low[...]), near], axis=0)
        return near, dot(parts[64:], chain_in[:, : count * EL])

    def spot(c, i):
        return pl.multiple_of(c * 512 + i * 64, 64)

    def block(c, i):
        return pl.ds(spot(c, i), 64)

    def across(ref, c, j):
        at = [pl.multiple_of(c * 512 + i * 64 + j * 8, 8) for i in range(8)]
        if ref.shape[1] == 128:
            return jnp.concatenate([ld(ref, one, 8) for one in at], axis=0)
        return jnp.concatenate([ref[pl.ds(one, 8), :] for one in at], axis=0)

    def put_across(ref, c, j, value):
        for i in range(8):
            at = pl.multiple_of(c * 512 + i * 64 + j * 8, 8)
            if ref.shape[1] == 128:
                st(ref, at, value[i * 8 : i * 8 + 8])
            else:
                ref[pl.ds(at, 8), :] = value[i * 8 : i * 8 + 8]

    lane = lax.broadcasted_iota(jnp.int32, (64, EL), 1)

    def chain_near(lead, tail):
        near0 = jnp.where(lane == 0, 0.0, pltpu.roll(tail, 1, 1))
        near1 = jnp.where(lane == EL - 1, 0.0, pltpu.roll(lead, EL - 1, 1))
        return near0, near1

    def side(v, parts, j):
        return jnp.concatenate(
            [ld(v, c * 512 + i * 64 + j * 8, 8) for c in parts for i in range(8)], axis=0
        )

    def low_faces(v):
        return low_message(side(v, (0, 1), 0), side(v, (0, 1), 7))

    def send_links(v, x, total):
        leads = [v[c * 512 : c * 512 + 64, :] for c in range(3)]
        tails = [v[1536 + c * 512 + 448 : 1536 + c * 512 + 512, :] for c in range(3)]
        fill_message(x, total, side(v, (2,), 0), side(v, (2,), 7), leads, tails)
        if x == 0:
            pl.semaphore_wait(
                barrier,
                leaves - 1 + (lobe > 0).astype(jnp.int32) + (lobe < lobes - 1).astype(jnp.int32),
            )
            for c in range(3):
                start_z(zs, zr, 0, 0, c)
        start_links(x)

    def advance(v, w):
        scale = 2.0 / size[...]
        visc = viscosity * scale
        step = time_step * scale

        def one(j, carry):
            for c in range(3):
                y = dot(table[ROW_IK : ROW_IK + 128, :192], stack(across(v, c, j)))
                put_across(part, c, j, across(base, 0, j) * y[:64] + visc * y[64:])
            return carry

        lax.fori_loop(0, 8, one, 0, unroll=4)
        sub = lax.broadcasted_iota(jnp.int32, (64, EL), 0)
        k, j = sub & 7, sub >> 3
        edge = ((k == 0) | (k == 7)).astype(F32) + ((j == 0) | (j == 7)).astype(F32)

        def two(i, carry):
            own = [ld(v, spot(r, i), 64) for r in range(3)]
            b1, b2 = base[block(1, i), :], base[block(2, i), :]
            ends = jnp.where((i == 0) | (i == 7), 1.0, 0.0).astype(F32)
            keep = 1.0 - penalty * (edge + ends)
            for c in range(3):
                y = dot(table[ROW_JK : ROW_JK + 192, :192], stack(own[c]))
                total = part[block(c, i), :] + b1 * y[:64] + b2 * y[64:128] + visc * y[128:]
                for r in range(3):
                    total -= own[r] * grads[block(c * 3 + r, i), :]
                st(w, spot(c, i), keep * own[c] + step * total)
            return carry

        lax.fori_loop(0, 8, two, 0, unroll=4)
        for c in range(3):
            near0, near1 = chain_near(ld(v, spot(c, 0), 64), ld(v, spot(c, 7), 64))
            add(w, spot(c, 0), penalty * near0)
            add(w, spot(c, 7), penalty * near1)
    def add_links(w, near, ends):
        for c in range(3):
            end = ends[:, c * EL : (c + 1) * EL]
            add(w, spot(c, 0), jnp.where(lane == 0, penalty * end, 0.0))
            add(w, spot(c, 7), jnp.where(lane == EL - 1, penalty * end, 0.0))
            for i in range(8):
                for f, j in ((0, 0), (1, 7)):
                    r0 = c * 64 + i * 8
                    add(
                        w, c * 512 + i * 64 + j * 8,
                        penalty * near[r0 : r0 + 8, f * EL : (f + 1) * EL],
                    )

    def add_z(w, x, c):
        for f, k in ((0, 0), (1, 7)):
            for h, at in enumerate(ends_of(w, c * 512, k)):
                here = slice(c * 64, c * 64 + 64), slice(h * 128, h * 128 + 128)
                value = w[at, :] + penalty * zr[x, f, here[0], here[1]]
                w[at, :] = value
                if x == 0:
                    zs[1, f, here[0], here[1]] = value

    for c in range(3):
        loads[1 + 2 * c].wait()
        loads[2 + 2 * c].wait()
        for f, k in ((0, 0), (1, 7)):
            for h, at in enumerate(ends_of(v0, c * 512, k)):
                zs[0, f, c * 64 : c * 64 + 64, h * 128 : h * 128 + 128] = v0[at, :]
    for load in loads[7:]:
        load.start()
    send_links(v0, 0, low_faces(v0))
    for load in loads[7:]:
        load.wait()

    def grad_one(j, carry):
        for r in range(3):
            y = dot(table[ROW_IK : ROW_IK + 64, :192], stack(across(base, r, j)))
            put_across(grads, r, j, y)
        return carry

    lax.fori_loop(0, 8, grad_one, 0, unroll=4)

    def grad_two(i, carry):
        for r in range(3):
            y = dot(table[ROW_JK : ROW_JK + 128, :192], stack(base[block(r, i), :]))
            grads[block(3 + r, i), :] = y[:64]
            grads[block(6 + r, i), :] = y[64:]
        return carry

    lax.fori_loop(0, 8, grad_two, 0, unroll=4)
    advance(v0, v1)
    wait_links(0, False)
    add_links(v1, *read_links(0, 3))
    total = None
    for c in range(3):
        wait_z(zs, zr, 0, 0, c, False)
        add_z(v1, 0, c)
        start_z(zs, zr, 1, 1, c)
        if c == 1:
            total = low_faces(v1)
    send_links(v1, 1, total)

    scale_square = (1.0 / size[...]) ** 2

    def recip_body(b, carry):
        at = pl.multiple_of(b * 8, 8)
        here = sums[pl.ds(at, 8), :]
        here = jnp.concatenate([here, here], axis=1)
        for m in range(10):
            recip[pl.ds(pl.multiple_of(m * MODES + at, 8), 8), :] = 1.0 / (
                (here + float(eigen[m])) * scale_square + shift_term
            )
        return carry

    lax.fori_loop(0, MODES // 8, recip_body, 0)
    advance(v1, v2)

    scale = 2.0 / size[...]

    def div_one(j, carry):
        put_across(res, 0, j, dot(table[ROW_IK : ROW_IK + 64, :192], stack(across(v2, 0, j))))
        return carry

    lax.fori_loop(0, 8, div_one, 0, unroll=4)

    def div_pair(first_part, second_part):
        both = jnp.concatenate([stack(first_part), stack(second_part)], axis=0)
        return dot(table[ROW_DIV : ROW_DIV + 64, :], both)

    def div_two(i, carry):
        add(res, spot(0, i), div_pair(ld(v2, spot(1, i), 64), ld(v2, spot(2, i), 64)))
        return carry

    lax.fori_loop(0, 8, div_two, 0, unroll=4)

    wait_links(1, False)
    near, ends = read_links(1, 3)
    end0 = [jnp.where(lane == 0, penalty * ends[:, c * EL : (c + 1) * EL], 0.0) for c in range(3)]
    end1 = [
        jnp.where(lane == EL - 1, penalty * ends[:, c * EL : (c + 1) * EL], 0.0) for c in range(3)
    ]
    ends_fix = {0: div_pair(end0[1], end0[2]), 7: div_pair(end1[1], end1[2])}
    for c in range(3):
        wait_z(zs, zr, 1, 1, c, False)

    def shell(c, f):
        here = slice(c * 64, c * 64 + 64)
        if f < 2:
            return penalty * near[here, f * EL : (f + 1) * EL]
        return penalty * zr[1, f - 2, here, :]

    shells = [[shell(c, f) for f in range(4)] for c in range(3)]
    along_i = [dot(table[ROW_IK : ROW_IK + 64, :192], stack(one)) for one in shells[0]]
    diff = node_tables()
    for i in range(8):
        r0 = slice(i * 8, i * 8 + 8)
        plane = jnp.concatenate([shells[c][f][r0] for c in (1, 2) for f in range(4)], axis=0)
        rest = split(jnp.concatenate([one[r0] for one in along_i], axis=0))
        y = dot(
            table[ROW_FIX : ROW_FIX + 64, :256], jnp.concatenate([stack(plane), *rest], axis=0)
        )
        y += float(diff[i, 0]) * end0[0] + float(diff[i, 7]) * end1[0]
        if i in ends_fix:
            y += ends_fix[i]
        st(res, i * 64, scale * (ld(res, i * 64, 64) + y))
    face2 = jnp.concatenate([ld(res, i * 64, 8) for i in range(8)], axis=0)
    face3 = jnp.concatenate([ld(res, i * 64 + 56, 8) for i in range(8)], axis=0)
    fill_message(2, None, face2, face3, [res[0:64, :]], [res[512 + 448 : 512 + 512, :]])
    start_links(2)
    for f, k in ((0, 0), (1, 7)):
        for h, at in enumerate(ends_of(res, 0, k)):
            zs1[0, f, :, h * 128 : h * 128 + 128] = res[at, :]
    start_z(zs1, zr1, 0, 2, 0)

    add_links(v2, near, ends)
    for c in range(3):
        add_z(v2, 1, c)
    out_copies = [
        pltpu.make_async_copy(
            v2.at[h * 1536 : h * 1536 + 1536], out_hbm.at[:, h * 128 : h * 128 + 128], out_sem.at[h]
        )
        for h in range(2)
    ]
    for copy in out_copies:
        copy.start()

    def forward(i, carry):
        y = dot(table[ROW_INT : ROW_INT + MODES16, :192], stack(ld(res, spot(0, i), 64)))
        modes[pl.ds(pl.multiple_of((i + 1) * MODES, 8), MODES), :] = y[:MODES]
        return carry

    lax.fori_loop(0, 8, forward, 0, unroll=4)
    near0, near1 = chain_near(ld(res, 0, 64), ld(res, 448, 64))
    wait_links(2, False)
    near, ends = read_links(2, 1)
    near0 = jnp.where(lane == 0, ends, near0)
    near1 = jnp.where(lane == EL - 1, ends, near1)
    for n, plane in ((0, near0), (9, near1)):
        y = dot(table[ROW_INT : ROW_INT + MODES16, :192], stack(plane))
        modes[n * MODES : (n + 1) * MODES, :] = y[:MODES]
    wait_z(zs1, zr1, 0, 2, 0, False)
    for i in range(8):
        r0 = slice(i * 8, i * 8 + 8)
        layer = jnp.concatenate(
            [near[r0, :EL], near[r0, EL:], zr1[0, 0, r0, :], zr1[0, 1, r0, :]], axis=0
        )
        y = dot(table[ROW_LAY : ROW_LAY + MODES16, :96], stack(layer))
        modes[(i + 1) * MODES : (i + 2) * MODES, :] += y[:MODES]

    along = table[ROW_ALONG : ROW_ALONG + 80, :240]

    def solve(b, carry):
        at = [pl.ds(pl.multiple_of(m * MODES + b * 8, 8), 8) for m in range(10)]
        values = jnp.concatenate([modes[one, :] for one in at], axis=0)
        values = dot(along, stack(values))
        values = values * jnp.concatenate([recip[one, :] for one in at], axis=0)
        values = dot(along, stack(values))
        for m in range(10):
            modes[at[m], :] = values[m * 8 : m * 8 + 8]
        return carry

    lax.fori_loop(0, MODES // 8, solve, 0, unroll=MODES // 8)

    pad = jnp.zeros((MODES16 - MODES, EL), F32)

    def mode_plane(n):
        plane = modes[pl.ds(pl.multiple_of(n * MODES, 8), MODES), :]
        return stack(jnp.concatenate([plane, pad], axis=0))

    for i in range(8):
        y = dot(table[ROW_BACK + 64 : ROW_BACK + 96, : 3 * MODES16], mode_plane(i + 1))
        r0 = slice(i * 8, i * 8 + 8)
        outer[128 + i * 8 : 136 + i * 8, :] = y[0:8]
        outer[192 + i * 8 : 200 + i * 8, :] = y[8:16]
        zs1[1, 0, r0, :] = y[16:24]
        zs1[1, 1, r0, :] = y[24:32]
    for n, at in ((0, 0), (9, 64)):
        outer[at : at + 64, :] = dot(table[ROW_BACK : ROW_BACK + 64, : 3 * MODES16], mode_plane(n))
    fill_message(
        3, None, outer[128:192, :], outer[192:256, :],
        [outer[0:64, 0:128]], [outer[64:128, 128:256]],
    )
    start_links(3)
    start_z(zs1, zr1, 1, 3, 0)

    def backward(i, carry):
        st(press, spot(0, i), dot(table[ROW_BACK : ROW_BACK + 64, : 3 * MODES16], mode_plane(i + 1)))
        return carry

    lax.fori_loop(0, 8, backward, 0, unroll=4)
    near0, near1 = chain_near(outer[0:64, :], outer[64:128, :])
    wait_links(3, False)
    near, ends = read_links(3, 1)
    add(press, 0, jnp.where(lane == 0, ends, near0))
    add(press, 448, jnp.where(lane == EL - 1, ends, near1))
    for i in range(8):
        for f, j in ((0, 0), (1, 7)):
            at = i * 64 + j * 8
            add(press, at, near[i * 8 : i * 8 + 8, f * EL : (f + 1) * EL])
    wait_z(zs1, zr1, 1, 3, 0, False)
    press_copies = []
    for h in range(2):
        for f, k in ((0, 0), (1, 7)):
            at = ends_of(press, 0, k)[h]
            press[at, :] = press[at, :] + zr1[1, f, :, h * 128 : h * 128 + 128]
        copy = pltpu.make_async_copy(
            press.at[h * 512 : h * 512 + 512], press_hbm.at[:, h * 128 : h * 128 + 128], out_sem.at[2 + h]
        )
        copy.start()
        press_copies.append(copy)
    for x in range(4):
        wait_links(x, True)
        if x < 2:
            for c in range(3):
                wait_z(zs, zr, x, x, c, True)
        else:
            wait_z(zs1, zr1, x - 2, x, 0, True)
    for copy in out_copies + press_copies:
        copy.wait()


def hand_over(first, second, first_out, second_out, sem):
    copies = []
    for q in range(PIECES):
        at = pl.ds(q * (1536 // PIECES), 1536 // PIECES)
        copies.append(pltpu.make_async_copy(first.at[at], first_out.at[at], sem.at[q]))
    copies.append(pltpu.make_async_copy(second, second_out, sem.at[PIECES]))
    for copy in copies:
        copy.start()
    for copy in copies:
        copy.wait()


def local(leaves, lobes, base_velocity, adjoint_velocity, element_size, link_slot):
    table, sums = constant_tables()
    rows = leaves * 8
    any_space = pl.BlockSpec(memory_space=pl.ANY)
    scratch = [
        pltpu.VMEM((1536, EL), F32),
        pltpu.VMEM((3072, 128), F32),
        pltpu.VMEM((3072, 128), F32),
        pltpu.VMEM((3072, 128), F32),
        pltpu.VMEM((9 * 512, EL), F32),
        pltpu.VMEM((1536, EL), F32),
        pltpu.VMEM((1024, 128), F32),
        pltpu.VMEM((10 * MODES, EL), F32),
        pltpu.VMEM((10 * MODES, EL), F32),
        pltpu.VMEM((1024, 128), F32),
        pltpu.VMEM((256, EL), F32),
        pltpu.VMEM((1, EL), F32),
        pltpu.VMEM((1, leaves * 4), jnp.int32),
        pltpu.VMEM((ROW_END, WIDE), BF16),
        pltpu.VMEM((MODES, 128), F32),
        pltpu.VMEM((2, 2, 192, EL), F32),
        pltpu.VMEM((2, 2, 192, EL), F32),
        pltpu.VMEM((2, 2, 64, EL), F32),
        pltpu.VMEM((2, 2, 64, EL), F32),
        pltpu.VMEM((4, rows, 128), F32),
        pltpu.VMEM((4, rows, 128), F32),
        pltpu.VMEM((rows, 1024), BF16),
        pltpu.VMEM((rows, 1792), BF16),
        pltpu.VMEM((2 * rows, 512), BF16),
        pltpu.VMEM((2 * rows, 512), BF16),
        pltpu.VMEM((2 * rows, 768), BF16),
        pltpu.SemaphoreType.DMA((11,)),
        pltpu.SemaphoreType.DMA((4,)),
        pltpu.SemaphoreType.DMA((4, 2, 3)),
        pltpu.SemaphoreType.DMA((4, 2, 3)),
        pltpu.SemaphoreType.DMA((4,)),
        pltpu.SemaphoreType.DMA((4,)),
    ]
    out, press = pl.pallas_call(
        functools.partial(kernel, leaves, lobes),
        out_shape=(
            jax.ShapeDtypeStruct((1536, EL), F32),
            jax.ShapeDtypeStruct((512, EL), F32),
        ),
        in_specs=[any_space] * 6,
        out_specs=(any_space, any_space),
        scratch_shapes=scratch,
        compiler_params=pltpu.CompilerParams(
            collective_id=0, has_side_effects=True, vmem_limit_bytes=40 * 1024 * 1024
        ),
    )(
        *[
            pltpu.with_memory_space_constraint(one, pltpu.HBM)
            for one in (
                base_velocity.reshape(1536, EL),
                adjoint_velocity.reshape(1536, EL),
                element_size.reshape(1, EL),
                link_slot.reshape(1, leaves * 4),
                jnp.asarray(table),
                jnp.asarray(sums),
            )
        ]
    )
    out, press = pl.pallas_call(
        hand_over,
        out_shape=(
            pltpu.HBM((1536, EL), F32),
            pltpu.HBM((512, EL), F32),
        ),
        in_specs=[any_space] * 2,
        out_specs=(any_space, any_space),
        scratch_shapes=[pltpu.SemaphoreType.DMA((PIECES + 1,))],
        compiler_params=pltpu.CompilerParams(vmem_limit_bytes=32 * 1024 * 1024),
    )(out, press)
    return out.reshape(3, 512, EL), press


def solution(mesh):
    placed = (
        P(None, None, ("leaf", "lobe")),
        P(None, None, ("leaf", "lobe")),
        P(("leaf", "lobe")),
        P(("leaf", "lobe")),
    )
    return jax.shard_map(
        functools.partial(local, mesh.shape["leaf"], mesh.shape["lobe"]),
        mesh=mesh,
        in_specs=placed,
        out_specs=(P(None, None, ("leaf", "lobe")), P(None, ("leaf", "lobe"))),
        check_vma=False,
    )
```
